32 devices in a mesh: pair: 2 (over y), src: 8 (over z, x), tgt: 2 (over core).
Axes of the slice: x: 2, y: 2, z: 4, core: 2. Of those that a mesh axis runs over, the one named last changes fastest.
Arguments:
- source_features: bfloat16 [64, 8, 256], P('pair', 'src'), parts along dimension 0, may hold values from -6 to 6
- target_features: bfloat16 [128, 8, 256], P(('pair', 'tgt'), 'src'), parts along dimension 0, may hold values from -6 to 6
- source_rows: int32 [8], P('pair'), parts along dimension 0, may hold values from 0 to 31
- target_cols: int32 [16], P('pair'), parts along dimension 0, may hold values from 0 to 7, each once
- target_kernel_one: bfloat16 [3, 3, 16, 16], replicated, may hold values from -0.75 to 0.75
- source_kernel: bfloat16 [3, 3, 16, 16], replicated, may hold values from -0.75 to 0.75
- target_kernel_two: bfloat16 [3, 3, 16, 16], replicated, may hold values from -0.75 to 0.75
Outputs:
- filtered: bfloat16 [8, 8, 64, 128], P('pair', 'src', 'tgt'), parts along dimension 0
The draws below stay inside these ranges and needn't reach their ends.
There are 2 independent parts, one for each index of `pair`. The reference program is written for one: setup_inputs(seed, part) draws one part's arguments, and reference() takes and returns one part's arrays. A program takes and returns all parts, laid end to end along the dimension named above; an argument that names none is the same for every part. Nothing has to cross between parts.
Inputs may be any that keep to these rules, and one draw needn't show every extreme that they name: `target_cols`: each column index appears once.
All inputs are finite; a program needn't handle non-finite values.
Results may differ from the reference program's by a relative error of at most 0.0074.
Values may be sent and summed in bfloat16 or wider, within the bound.
A program may use at most 128 MiB of HBM per device.

```python
import jax
import jax.numpy as jnp
from jax import lax

HS_MAP = 32
HS = 4
HT = 64
F = 256
G = 16
WS = 8
WT = 8


def place_ends(drawn, stream_key, smallest, high):
    place = [jax.random.randint(jax.random.fold_in(stream_key, axis), (), 0, length) for axis, length in enumerate(drawn.shape)]
    widest = drawn.shape.index(max(drawn.shape))
    beside = place[:widest] + [(place[widest] + 1) % drawn.shape[widest]] + place[widest + 1:]
    return drawn.at[tuple(place)].set(smallest).at[tuple(beside)].set(high)


def level_of(rng, dims, cuts, least, high):
    loudness = 1.0
    for position, parts in cuts:
        steps = jax.random.uniform(jax.random.fold_in(jax.random.fold_in(rng, 6), position), (parts,), jnp.float32, least / len(cuts), high / len(cuts))
        loudness = loudness * jnp.repeat(jnp.exp(steps), dims[position] // parts).reshape((-1,) + (1,) * (len(dims) - 1 - position))
    return loudness


def bell_draw(own_key, shape, width, reach, pieces=(), held_as=jnp.bfloat16):
    entries = width * jax.random.normal(own_key, shape, jnp.float32)
    if pieces:
        entries = entries * level_of(own_key, shape, pieces, -0.22, 0.18)
    return jnp.clip(entries, -reach, reach).astype(held_as)


def setup_inputs(seed: int = 0, part: int = 0) -> dict:
    seeds = jax.random.split(jax.random.key(seed), 8)
    part_splits = jax.random.split(jax.random.fold_in(seeds[7], part), 8)
    source_features = bell_draw(part_splits[0], (HS_MAP, WS, F), 1.0, 6.0, ((1, 8),))
    target_features = bell_draw(part_splits[1], (HT, WT, F), 1.0, 6.0, ((0, 2), (1, 8)))
    source_rows = place_ends(jax.random.randint(part_splits[2], (HS,), 0, HS_MAP), jax.random.fold_in(part_splits[2], 1), 0, HS_MAP - 1).astype(jnp.int32)
    target_cols = jax.random.permutation(part_splits[3], WT).astype(jnp.int32)
    target_kernel_one = bell_draw(seeds[4], (3, 3, G, G), (9 * G // 2) ** -0.5, 0.75)
    source_kernel = bell_draw(seeds[5], (3, 3, G, G), (9 * G // 2) ** -0.5, 0.75)
    target_kernel_two = bell_draw(seeds[6], (3, 3, G, G), (9 * G // 2) ** -0.5, 0.75)
    return dict(source_features=source_features, target_features=target_features, source_rows=source_rows, target_cols=target_cols, target_kernel_one=target_kernel_one, source_kernel=source_kernel, target_kernel_two=target_kernel_two)


def plane_filter(plane_slice, kernel):
    height = plane_slice.shape[0]
    breadth = plane_slice.shape[1]
    padded = jnp.pad(plane_slice, ((1, 1), (1, 1), (0, 0)))
    running = jnp.zeros((height, breadth, kernel.shape[3]), jnp.float32)
    for offset_y in range(3):
        for offset_x in range(3):
            running = running + jnp.einsum('abi,io->abo', padded[offset_y:offset_y + height, offset_x:offset_x + breadth], kernel[offset_y, offset_x], precision=lax.Precision.HIGHEST)
    return jnp.maximum(running, 0.0).astype(jnp.bfloat16)


def target_section(volume, kernel):
    groups = volume.shape[4]
    flattened = volume.reshape(HS * WS, HT, WT, groups)
    result = lax.map(lambda plane_slice: plane_filter(plane_slice.astype(jnp.float32), kernel), flattened)
    return result.reshape(HS, WS, HT, WT, groups)


def source_section(volume, kernel):
    groups = volume.shape[4]
    reordered = volume.transpose(2, 3, 0, 1, 4).reshape(HT * WT, HS, WS, groups)
    result = lax.map(lambda plane_slice: plane_filter(plane_slice.astype(jnp.float32), kernel), reordered)
    return result.reshape(HT, WT, HS, WS, groups).transpose(2, 3, 0, 1, 4)


def reference(source_features, target_features, source_rows, target_cols, target_kernel_one, source_kernel, target_kernel_two):
    groups = target_kernel_one.shape[2]
    channels = source_features.shape[2] // groups
    src_window = jnp.take(source_features, source_rows.astype(jnp.int32), axis=0)
    tgt_window = jnp.take(target_features, target_cols.astype(jnp.int32), axis=1)
    source_grouped = src_window.astype(jnp.float32).reshape(HS, WS, groups, channels)
    target_grouped = tgt_window.astype(jnp.float32).reshape(HT, WT, groups, channels)
    volume = jnp.einsum('hsgc,rwgc->hsrwg', source_grouped, target_grouped, precision=lax.Precision.HIGHEST)
    volume = (volume * (channels ** -0.5)).astype(jnp.bfloat16)
    section_one = target_section(volume, target_kernel_one.astype(jnp.float32))
    section_two = source_section(section_one, source_kernel.astype(jnp.float32))
    section_three = target_section(section_two, target_kernel_two.astype(jnp.float32))
    return section_three.reshape(HS, WS, HT, WT * groups)
```

```python
import functools

import jax
import jax.numpy as jnp
from jax import lax
from jax.experimental import pallas as pl
from jax.experimental.pallas import tpu as pltpu
from jax.sharding import PartitionSpec as P

MESH = pl.DeviceIdType.MESH
LANES = 128
HALO = 16
BF16 = jnp.bfloat16
F32 = jnp.float32


def iota(shape, dim):
    return lax.broadcasted_iota(jnp.int32, shape, dim)


def dot(a, b):
    return jnp.dot(a, b, preferred_element_type=F32)


def kernel(
    src_count,
    tgt_count,
    breadth,
    window_rows,
    groups,
    rows_ref,
    cols_ref,
    tgt_hbm,
    src_hbm,
    k1_hbm,
    ks_hbm,
    k2_hbm,
    out_ref,
    buf,
    sbuf,
    taps,
    vol,
    sec,
    stage,
    w1,
    w2,
    w3,
    local_sem,
    send_sem,
    recv_sem,
    halo_send,
    halo_recv,
    src_send,
    src_recv,
):
    rows, features = tgt_hbm.shape
    map_rows = src_hbm.shape[0]
    channels = features // groups
    span = rows + HALO
    width = vol.shape[1]
    column_lanes = window_rows * groups
    per_block = LANES // groups
    chunks = breadth // per_block
    chunk_rows = per_block * span
    me = lax.axis_index("src")
    half = lax.axis_index("tgt")
    main = pl.ds(pl.multiple_of(half * HALO, HALO), rows)

    def peer(d):
        return lax.rem(me + d, src_count)

    barrier = pltpu.get_barrier_semaphore()
    for d in range(1, src_count):
        pl.semaphore_signal(barrier, inc=1, device_id={"src": peer(d)}, device_id_type=MESH)
    if tgt_count > 1:
        pl.semaphore_signal(barrier, inc=1, device_id={"tgt": 1 - half}, device_id_type=MESH)

    own = [
        pltpu.make_async_copy(tgt_hbm, buf.at[me, main], local_sem.at[0]),
        pltpu.make_async_copy(src_hbm, sbuf.at[1], local_sem.at[1]),
        pltpu.make_async_copy(k1_hbm, taps.at[0], local_sem.at[2]),
        pltpu.make_async_copy(ks_hbm, taps.at[1], local_sem.at[3]),
        pltpu.make_async_copy(k2_hbm, taps.at[2], local_sem.at[4]),
    ]
    for copy in own:
        copy.start()
    pl.semaphore_wait(barrier, src_count - 1 + (1 if tgt_count > 1 else 0))

    edge = pl.ds(pl.multiple_of(half * HALO + (1 - half) * (rows - HALO), HALO), HALO)
    landing = pl.ds(pl.multiple_of(half * rows, HALO), HALO)

    to_right = pltpu.make_async_remote_copy(
        src_ref=src_hbm, dst_ref=sbuf.at[0], send_sem=src_send.at[0], recv_sem=src_recv.at[0],
        device_id={"src": lax.rem(me + 1, src_count)}, device_id_type=MESH,
    )
    to_left = pltpu.make_async_remote_copy(
        src_ref=src_hbm, dst_ref=sbuf.at[2], send_sem=src_send.at[1], recv_sem=src_recv.at[1],
        device_id={"src": lax.rem(me + src_count - 1, src_count)}, device_id_type=MESH,
    )
    sends = []
    for d in range(1, src_count):
        sends.append(
            pltpu.make_async_remote_copy(
                src_ref=tgt_hbm, dst_ref=buf.at[me, main], send_sem=send_sem.at[d],
                recv_sem=recv_sem.at[d], device_id={"src": peer(d)}, device_id_type=MESH,
            )
        )
    order = sorted(range(1, src_count), key=lambda d: -min(d, src_count - d))
    for d in order:
        sends[d - 1].start()
    to_right.start()
    to_left.start()

    def forward(d, source):
        column = lax.rem(me + src_count - d, src_count)
        return pltpu.make_async_remote_copy(
            src_ref=source(column), dst_ref=buf.at[column, landing], send_sem=halo_send.at[d],
            recv_sem=halo_recv.at[d], device_id={"tgt": 1 - half}, device_id_type=MESH,
        )

    forwards = []
    if tgt_count > 1:
        offset = pl.multiple_of((1 - half) * (rows - HALO), HALO)
        forwards.append(forward(0, lambda column: tgt_hbm.at[pl.ds(offset, HALO)]))
        forwards[0].start()

    zero_block = jnp.zeros((span, width), BF16)
    for ref in (vol, sec):
        ref[pl.ds(0, span), :] = zero_block
        ref[pl.ds((breadth + 1) * span, span), :] = zero_block
    for copy in own[2:]:
        copy.wait()
    expand = (iota((groups, width), 1) % groups == iota((groups, width), 0)).astype(BF16)
    spread = [dot(taps[i], expand).astype(BF16) for i in range(3)]
    lane_group = iota((groups, width), 1) // groups
    nothing = jnp.zeros((groups, width), BF16)

    def tap(i, a, b):
        start = (a * 3 + b) * groups
        return spread[i][start : start + groups]

    for a in range(3):
        for b in range(3):
            for j in range(width // groups):
                w1[a, pl.ds(b * width + j * groups, groups), :] = jnp.where(
                    lane_group == j, tap(0, a, b), nothing
                )
    for j in range(width // groups):
        k, h = divmod(j, window_rows)
        two = nothing
        three = [nothing[:, :LANES]] * 3
        if k < 3:
            for a in range(3):
                two = jnp.where(lane_group % window_rows == h - a + 1, tap(1, a, k), two)
                three[a] = jnp.where(
                    (lane_group % window_rows == h)[:, :LANES], tap(2, a, k)[:, :LANES], three[a]
                )
        w2[pl.ds(j * groups, groups), :] = two
        for a in range(3):
            w3[pl.ds(j * groups, groups), pl.ds(a * LANES, LANES)] = three[a]

    def valid(extra):
        position = iota((chunk_rows, width), 0) % span
        low = half * (HALO - extra)
        return (position >= low) & (position < low + rows + extra)

    own[1].wait()
    to_right.wait()
    to_left.wait()
    row_of = iota((column_lanes, map_rows), 0) // groups
    wanted = jnp.zeros((column_lanes, map_rows), jnp.int32)
    for h in range(window_rows):
        wanted = jnp.where(row_of == h, rows_ref[h], wanted)
    select = (iota((column_lanes, map_rows), 1) == wanted).astype(BF16)
    same_group = (
        iota((column_lanes, features), 1) // channels == iota((column_lanes, features), 0) % groups
    )
    parts = []
    for k in range(3):
        keep = same_group
        if k == 0:
            keep = keep & (me > 0)
        if k == 2:
            keep = keep & (me < src_count - 1)
        parts.append(jnp.where(keep, dot(select, sbuf[k]), 0.0).astype(BF16))
    if width > 3 * column_lanes:
        parts.append(jnp.zeros((width - 3 * column_lanes, features), BF16))
    weights = jnp.concatenate(parts, axis=0)

    own[0].wait()
    for d in range(1, src_count):
        sends[d - 1].wait_recv()
        if tgt_count > 1:
            copy = forward(d, lambda column: buf.at[column, edge])
            copy.start()
            forwards.append(copy)
    for copy in forwards:
        copy.wait_recv()

    def volume_chunk(chunk):
        window = jnp.concatenate(
            [buf[cols_ref[chunk * per_block + i]] for i in range(per_block)], axis=0
        )
        scores = lax.dot_general(
            window, weights, (((1,), (1,)), ((), ())), preferred_element_type=F32
        ) * (channels ** -0.5)
        vol[pl.ds(pl.multiple_of((chunk * per_block + 1) * span, span), chunk_rows), :] = (
            jnp.where(valid(2), scores, 0.0).astype(BF16)
        )

    def at(chunk, b):
        return pl.ds(pl.multiple_of((chunk * per_block + b) * span, span), chunk_rows)

    def shifted(parts):
        total = parts[1] + pltpu.roll(parts[0], 1, 0)
        return total + pltpu.roll(parts[2], chunk_rows - 1, 0)

    def middle_chunk(chunk):
        window = jnp.concatenate([vol[at(chunk, b), :] for b in range(3)], axis=1)
        one = shifted([dot(window, w1[a]) for a in range(3)])
        one = jnp.maximum(one, 0.0).astype(BF16)
        two = jnp.maximum(dot(one, w2[...]), 0.0)
        sec[at(chunk, 1), :] = jnp.where(valid(1), two, 0.0).astype(BF16)

    def last_chunk(chunk):
        which = iota((chunk_rows, width), 1) // column_lanes
        window = jnp.where(
            which == 0,
            sec[at(chunk, 0), :],
            jnp.where(which == 1, sec[at(chunk, 1), :], sec[at(chunk, 2), :]),
        )
        three = dot(window, w3[...])
        three = shifted([three[:, a * LANES : (a + 1) * LANES] for a in range(3)])
        stage[...] = jnp.maximum(three, 0.0)
        pieces = [
            stage[pl.ds(pl.multiple_of(i * span + half * HALO, HALO), rows), :]
            for i in range(per_block)
        ]
        group = iota((rows, LANES), 1) // groups
        rolled = []
        for d in range(window_rows):
            mixed = pieces[d % per_block]
            for j in range(1, per_block):
                mixed = jnp.where(group == j, pieces[(j + d) % per_block], mixed)
            rolled.append(pltpu.roll(mixed, d * groups, 1) if d else mixed)
        for h in range(window_rows):
            total = rolled[0]
            for d in range(1, window_rows):
                total = jnp.where((group - h) % window_rows == d, rolled[d], total)
            out_ref[h, :, pl.ds(pl.multiple_of(chunk * LANES, LANES), LANES)] = total.astype(BF16)

    for step in (volume_chunk, middle_chunk, last_chunk):
        if chunks == 1:
            step(0)
        else:
            pl.loop(0, chunks)(step)

    for copy in sends:
        copy.wait_send()
    for copy in forwards:
        copy.wait_send()


def local(
    src_count,
    tgt_count,
    source_features,
    target_features,
    source_rows,
    target_cols,
    target_kernel_one,
    source_kernel,
    target_kernel_two,
):
    groups = source_kernel.shape[2]
    window_rows = source_rows.shape[0]
    breadth = target_cols.shape[0]
    map_rows, _, features = source_features.shape
    rows = target_features.shape[0]
    span = rows + HALO
    width = -(-3 * window_rows * groups // LANES) * LANES
    chunk_rows = LANES // groups * span
    taps = 9 * groups
    any_spec = pl.BlockSpec(memory_space=pl.ANY)
    smem = pl.BlockSpec(memory_space=pltpu.SMEM)
    dma = pltpu.SemaphoreType.DMA
    out = pl.pallas_call(
        functools.partial(kernel, src_count, tgt_count, breadth, window_rows, groups),
        out_shape=jax.ShapeDtypeStruct((window_rows, rows, breadth * groups), BF16),
        in_specs=[smem, smem] + [any_spec] * 5,
        out_specs=pl.BlockSpec(memory_space=pltpu.VMEM),
        scratch_shapes=[
            pltpu.VMEM((breadth, span, features), BF16),
            pltpu.VMEM((3, map_rows, features), BF16),
            pltpu.VMEM((3, taps, groups), BF16),
            pltpu.VMEM(((breadth + 2) * span, width), BF16),
            pltpu.VMEM(((breadth + 2) * span, width), BF16),
            pltpu.VMEM((chunk_rows, LANES), F32),
            pltpu.VMEM((3, 3 * width, width), BF16),
            pltpu.VMEM((width, width), BF16),
            pltpu.VMEM((width, 3 * LANES), BF16),
            dma((5,)),
            dma((src_count,)),
            dma((src_count,)),
            dma((src_count,)),
            dma((src_count,)),
            dma((2,)),
            dma((2,)),
        ],
        compiler_params=pltpu.CompilerParams(
            collective_id=0, has_side_effects=True, vmem_limit_bytes=48 * 1024 * 1024
        ),
    )(
        source_rows,
        target_cols,
        target_features[:, 0],
        source_features[:, 0],
        target_kernel_one.reshape(taps, groups),
        source_kernel.reshape(taps, groups),
        target_kernel_two.reshape(taps, groups),
    )
    return out[:, None]


def solution(mesh):
    return jax.shard_map(
        functools.partial(local, mesh.shape["src"], mesh.shape["tgt"]),
        mesh=mesh,
        in_specs=(
            P("pair", "src", None),
            P(("pair", "tgt"), "src", None),
            P("pair"),
            P("pair"),
            P(),
            P(),
            P(),
        ),
        out_specs=P("pair", "src", "tgt", None),
        check_vma=False,
    )
```

```python
import functools

import jax
import jax.numpy as jnp
from jax import lax
from jax.experimental import pallas as pl
from jax.experimental.pallas import tpu as pltpu
from jax.sharding import PartitionSpec as P

MESH = pl.DeviceIdType.MESH
LANES = 128
HALO = 16
BF16 = jnp.bfloat16
F32 = jnp.float32


def iota(shape, dim):
    return lax.broadcasted_iota(jnp.int32, shape, dim)


def dot(a, b):
    return jnp.dot(a, b, preferred_element_type=F32)


def kernel(
    src_count,
    tgt_count,
    breadth,
    window_rows,
    groups,
    rows_hbm,
    cols_hbm,
    tgt_hbm,
    src_hbm,
    k1_hbm,
    ks_hbm,
    k2_hbm,
    out_ref,
    rows_ref,
    cols_ref,
    buf,
    sbuf,
    taps,
    vol,
    sec,
    stage,
    w1,
    w2,
    w3,
    local_sem,
    send_sem,
    recv_sem,
    halo_send,
    halo_recv,
    src_send,
    src_recv,
):
    rows, features = tgt_hbm.shape
    map_rows = src_hbm.shape[0]
    channels = features // groups
    span = rows + HALO
    width = vol.shape[1]
    column_lanes = window_rows * groups
    per_block = LANES // groups
    chunks = breadth // per_block
    chunk_rows = per_block * span
    me = lax.axis_index("src")
    half = lax.axis_index("tgt")
    main = pl.ds(pl.multiple_of(half * HALO, HALO), rows)

    def peer(d):
        return lax.rem(me + d, src_count)

    barrier = pltpu.get_barrier_semaphore()
    for d in range(1, src_count):
        pl.semaphore_signal(barrier, inc=1, device_id={"src": peer(d)}, device_id_type=MESH)
    if tgt_count > 1:
        pl.semaphore_signal(barrier, inc=1, device_id={"tgt": 1 - half}, device_id_type=MESH)

    own = [
        pltpu.make_async_copy(tgt_hbm, buf.at[me, main], local_sem.at[0]),
        pltpu.make_async_copy(src_hbm, sbuf.at[1], local_sem.at[1]),
        pltpu.make_async_copy(k1_hbm, taps.at[0], local_sem.at[2]),
        pltpu.make_async_copy(ks_hbm, taps.at[1], local_sem.at[3]),
        pltpu.make_async_copy(k2_hbm, taps.at[2], local_sem.at[4]),
        pltpu.make_async_copy(rows_hbm, rows_ref, local_sem.at[5]),
        pltpu.make_async_copy(cols_hbm, cols_ref, local_sem.at[6]),
    ]
    for copy in own:
        copy.start()
    pl.semaphore_wait(barrier, src_count - 1 + (1 if tgt_count > 1 else 0))

    edge = pl.ds(pl.multiple_of(half * HALO + (1 - half) * (rows - HALO), HALO), HALO)
    landing = pl.ds(pl.multiple_of(half * rows, HALO), HALO)

    to_right = pltpu.make_async_remote_copy(
        src_ref=src_hbm, dst_ref=sbuf.at[0], send_sem=src_send.at[0], recv_sem=src_recv.at[0],
        device_id={"src": lax.rem(me + 1, src_count)}, device_id_type=MESH,
    )
    to_left = pltpu.make_async_remote_copy(
        src_ref=src_hbm, dst_ref=sbuf.at[2], send_sem=src_send.at[1], recv_sem=src_recv.at[1],
        device_id={"src": lax.rem(me + src_count - 1, src_count)}, device_id_type=MESH,
    )
    sends = []
    for d in range(1, src_count):
        sends.append(
            pltpu.make_async_remote_copy(
                src_ref=tgt_hbm, dst_ref=buf.at[me, main], send_sem=send_sem.at[d],
                recv_sem=recv_sem.at[d], device_id={"src": peer(d)}, device_id_type=MESH,
            )
        )
    order = sorted(range(1, src_count), key=lambda d: -min(d, src_count - d))
    to_right.start()
    to_left.start()
    for d in order:
        sends[d - 1].start()

    def forward(d, source):
        column = lax.rem(me + src_count - d, src_count)
        return pltpu.make_async_remote_copy(
            src_ref=source(column), dst_ref=buf.at[column, landing], send_sem=halo_send.at[d],
            recv_sem=halo_recv.at[d], device_id={"tgt": 1 - half}, device_id_type=MESH,
        )

    forwards = []
    if tgt_count > 1:
        offset = pl.multiple_of((1 - half) * (rows - HALO), HALO)
        forwards.append(forward(0, lambda column: tgt_hbm.at[pl.ds(offset, HALO)]))
        forwards[0].start()

    zero_block = jnp.zeros((span, width), BF16)
    for ref in (vol, sec):
        ref[pl.ds(0, span), :] = zero_block
        ref[pl.ds((breadth + 1) * span, span), :] = zero_block
    for copy in own[2:5]:
        copy.wait()
    expand = (iota((groups, width), 1) % groups == iota((groups, width), 0)).astype(BF16)
    spread = [dot(taps[i], expand).astype(BF16) for i in range(3)]
    lane_group = iota((groups, width), 1) // groups
    nothing = jnp.zeros((groups, width), BF16)

    def tap(i, a, b):
        start = (a * 3 + b) * groups
        return spread[i][start : start + groups]

    for a in range(3):
        for b in range(3):
            for j in range(width // groups):
                w1[a, pl.ds(b * width + j * groups, groups), :] = jnp.where(
                    lane_group == j, tap(0, a, b), nothing
                )
    for j in range(width // groups):
        k, h = divmod(j, window_rows)
        two = nothing
        three = [nothing[:, :LANES]] * 3
        if k < 3:
            for a in range(3):
                two = jnp.where(lane_group % window_rows == h - a + 1, tap(1, a, k), two)
                three[a] = jnp.where(
                    (lane_group % window_rows == h)[:, :LANES], tap(2, a, k)[:, :LANES], three[a]
                )
        w2[pl.ds(j * groups, groups), :] = two
        for a in range(3):
            w3[pl.ds(j * groups, groups), pl.ds(a * LANES, LANES)] = three[a]

    def valid(extra):
        position = iota((chunk_rows, width), 0) % span
        low = half * (HALO - extra)
        return (position >= low) & (position < low + rows + extra)

    own[1].wait()
    own[5].wait()
    own[6].wait()
    to_right.wait()
    to_left.wait()
    row_of = iota((column_lanes, map_rows), 0) // groups
    wanted = jnp.zeros((column_lanes, map_rows), jnp.int32)
    for h in range(window_rows):
        wanted = jnp.where(row_of == h, rows_ref[h], wanted)
    select = (iota((column_lanes, map_rows), 1) == wanted).astype(BF16)
    same_group = (
        iota((column_lanes, features), 1) // channels == iota((column_lanes, features), 0) % groups
    )
    parts = []
    for k in range(3):
        keep = same_group
        if k == 0:
            keep = keep & (me > 0)
        if k == 2:
            keep = keep & (me < src_count - 1)
        parts.append(jnp.where(keep, dot(select, sbuf[k]), 0.0).astype(BF16))
    if width > 3 * column_lanes:
        parts.append(jnp.zeros((width - 3 * column_lanes, features), BF16))
    weights = jnp.concatenate(parts, axis=0)

    own[0].wait()
    for d in range(1, src_count):
        sends[d - 1].wait_recv()
        if tgt_count > 1:
            copy = forward(d, lambda column: buf.at[column, edge])
            copy.start()
            forwards.append(copy)
    for copy in forwards:
        copy.wait_recv()

    def volume_chunk(chunk):
        window = jnp.concatenate(
            [buf[cols_ref[chunk * per_block + i]] for i in range(per_block)], axis=0
        )
        scores = lax.dot_general(
            window, weights, (((1,), (1,)), ((), ())), preferred_element_type=F32
        ) * (channels ** -0.5)
        vol[pl.ds(pl.multiple_of((chunk * per_block + 1) * span, span), chunk_rows), :] = (
            jnp.where(valid(2), scores, 0.0).astype(BF16)
        )

    def at(chunk, b):
        return pl.ds(pl.multiple_of((chunk * per_block + b) * span, span), chunk_rows)

    def shifted(parts):
        total = parts[1] + pltpu.roll(parts[0], 1, 0)
        return total + pltpu.roll(parts[2], chunk_rows - 1, 0)

    def middle_chunk(chunk):
        window = jnp.concatenate([vol[at(chunk, b), :] for b in range(3)], axis=1)
        one = shifted([dot(window, w1[a]) for a in range(3)])
        one = jnp.maximum(one, 0.0).astype(BF16)
        two = jnp.maximum(dot(one, w2[...]), 0.0)
        sec[at(chunk, 1), :] = jnp.where(valid(1), two, 0.0).astype(BF16)

    def last_chunk(chunk):
        which = iota((chunk_rows, width), 1) // column_lanes
        window = jnp.where(
            which == 0,
            sec[at(chunk, 0), :],
            jnp.where(which == 1, sec[at(chunk, 1), :], sec[at(chunk, 2), :]),
        )
        three = dot(window, w3[...])
        three = shifted([three[:, a * LANES : (a + 1) * LANES] for a in range(3)])
        stage[...] = jnp.maximum(three, 0.0)
        pieces = [
            stage[pl.ds(pl.multiple_of(i * span + half * HALO, HALO), rows), :]
            for i in range(per_block)
        ]
        group = iota((rows, LANES), 1) // groups
        rolled = []
        for d in range(window_rows):
            mixed = pieces[d % per_block]
            for j in range(1, per_block):
                mixed = jnp.where(group == j, pieces[(j + d) % per_block], mixed)
            rolled.append(pltpu.roll(mixed, d * groups, 1) if d else mixed)
        for h in range(window_rows):
            total = rolled[0]
            for d in range(1, window_rows):
                total = jnp.where((group - h) % window_rows == d, rolled[d], total)
            out_ref[h, :, pl.ds(pl.multiple_of(chunk * LANES, LANES), LANES)] = total.astype(BF16)

    for step in (volume_chunk, middle_chunk, last_chunk):
        if chunks == 1:
            step(0)
        else:
            pl.loop(0, chunks)(step)

    for copy in sends:
        copy.wait_send()
    for copy in forwards:
        copy.wait_send()


def local(
    src_count,
    tgt_count,
    source_features,
    target_features,
    source_rows,
    target_cols,
    target_kernel_one,
    source_kernel,
    target_kernel_two,
):
    groups = source_kernel.shape[2]
    window_rows = source_rows.shape[0]
    breadth = target_cols.shape[0]
    map_rows, _, features = source_features.shape
    rows = target_features.shape[0]
    span = rows + HALO
    width = -(-3 * window_rows * groups // LANES) * LANES
    chunk_rows = LANES // groups * span
    taps = 9 * groups
    hbm = pl.BlockSpec(memory_space=pltpu.HBM)
    dma = pltpu.SemaphoreType.DMA
    out = pl.pallas_call(
        functools.partial(kernel, src_count, tgt_count, breadth, window_rows, groups),
        out_shape=jax.ShapeDtypeStruct((window_rows, rows, breadth * groups), BF16),
        in_specs=[hbm] * 7,
        out_specs=pl.BlockSpec(memory_space=pltpu.VMEM),
        scratch_shapes=[
            pltpu.SMEM((window_rows,), jnp.int32),
            pltpu.SMEM((breadth,), jnp.int32),
            pltpu.VMEM((breadth, span, features), BF16),
            pltpu.VMEM((3, map_rows, features), BF16),
            pltpu.VMEM((3, taps, groups), BF16),
            pltpu.VMEM(((breadth + 2) * span, width), BF16),
            pltpu.VMEM(((breadth + 2) * span, width), BF16),
            pltpu.VMEM((chunk_rows, LANES), F32),
            pltpu.VMEM((3, 3 * width, width), BF16),
            pltpu.VMEM((width, width), BF16),
            pltpu.VMEM((width, 3 * LANES), BF16),
            dma((7,)),
            dma((src_count,)),
            dma((src_count,)),
            dma((src_count,)),
            dma((src_count,)),
            dma((2,)),
            dma((2,)),
        ],
        compiler_params=pltpu.CompilerParams(
            collective_id=0, has_side_effects=True, vmem_limit_bytes=48 * 1024 * 1024
        ),
    )(
        source_rows,
        target_cols,
        target_features[:, 0],
        source_features[:, 0],
        target_kernel_one.reshape(taps, groups),
        source_kernel.reshape(taps, groups),
        target_kernel_two.reshape(taps, groups),
    )
    return out[:, None]


def solution(mesh):
    return jax.shard_map(
        functools.partial(local, mesh.shape["src"], mesh.shape["tgt"]),
        mesh=mesh,
        in_specs=(
            P("pair", "src", None),
            P(("pair", "tgt"), "src", None),
            P("pair"),
            P("pair"),
            P(),
            P(),
            P(),
        ),
        out_specs=P("pair", "src", "tgt", None),
        check_vma=False,
    )
```

```python
import functools

import jax
import jax.numpy as jnp
from jax import lax
from jax.experimental import pallas as pl
from jax.experimental.pallas import tpu as pltpu
from jax.sharding import PartitionSpec as P

MESH = pl.DeviceIdType.MESH
LANES = 128
HALO = 16
BF16 = jnp.bfloat16
F32 = jnp.float32


def iota(shape, dim):
    return lax.broadcasted_iota(jnp.int32, shape, dim)


def dot(a, b):
    return jnp.dot(a, b, preferred_element_type=F32)


def kernel(
    src_count,
    tgt_count,
    breadth,
    window_rows,
    groups,
    rows_hbm,
    cols_hbm,
    tgt_hbm,
    src_hbm,
    k1_hbm,
    ks_hbm,
    k2_hbm,
    out_ref,
    rows_ref,
    cols_ref,
    buf,
    sbuf,
    taps,
    vol,
    sec,
    stage,
    w1,
    w2,
    w3,
    local_sem,
    send_sem,
    recv_sem,
    halo_send,
    halo_recv,
    src_send,
    src_recv,
):
    rows, features = tgt_hbm.shape
    map_rows = src_hbm.shape[0]
    channels = features // groups
    span = rows + HALO
    width = vol.shape[1]
    column_lanes = window_rows * groups
    per_block = LANES // groups
    chunks = breadth // per_block
    chunk_rows = per_block * span
    me = lax.axis_index("src")
    half = lax.axis_index("tgt")
    main = pl.ds(pl.multiple_of(half * HALO, HALO), rows)

    def peer(d):
        return lax.rem(me + d, src_count)

    barrier = pltpu.get_barrier_semaphore()
    for d in range(1, src_count):
        pl.semaphore_signal(barrier, inc=1, device_id={"src": peer(d)}, device_id_type=MESH)
    if tgt_count > 1:
        pl.semaphore_signal(barrier, inc=1, device_id={"tgt": 1 - half}, device_id_type=MESH)

    own = [
        pltpu.make_async_copy(tgt_hbm, buf.at[me, main], local_sem.at[0]),
        pltpu.make_async_copy(src_hbm, sbuf.at[1], local_sem.at[1]),
        pltpu.make_async_copy(k1_hbm, taps.at[0], local_sem.at[2]),
        pltpu.make_async_copy(ks_hbm, taps.at[1], local_sem.at[3]),
        pltpu.make_async_copy(k2_hbm, taps.at[2], local_sem.at[4]),
        pltpu.make_async_copy(rows_hbm, rows_ref, local_sem.at[5]),
        pltpu.make_async_copy(cols_hbm, cols_ref, local_sem.at[6]),
    ]
    for copy in own:
        copy.start()
    pl.semaphore_wait(barrier, src_count - 1 + (1 if tgt_count > 1 else 0))

    edge = pl.ds(pl.multiple_of(half * HALO + (1 - half) * (rows - HALO), HALO), HALO)
    landing = pl.ds(pl.multiple_of(half * rows, HALO), HALO)

    to_right = pltpu.make_async_remote_copy(
        src_ref=src_hbm, dst_ref=sbuf.at[0], send_sem=src_send.at[0], recv_sem=src_recv.at[0],
        device_id={"src": lax.rem(me + 1, src_count)}, device_id_type=MESH,
    )
    to_left = pltpu.make_async_remote_copy(
        src_ref=src_hbm, dst_ref=sbuf.at[2], send_sem=src_send.at[1], recv_sem=src_recv.at[1],
        device_id={"src": lax.rem(me + src_count - 1, src_count)}, device_id_type=MESH,
    )
    sends = []
    for d in range(1, src_count):
        sends.append(
            pltpu.make_async_remote_copy(
                src_ref=tgt_hbm, dst_ref=buf.at[me, main], send_sem=send_sem.at[d],
                recv_sem=recv_sem.at[d], device_id={"src": peer(d)}, device_id_type=MESH,
            )
        )
    order = sorted(range(1, src_count), key=lambda d: -min(d, src_count - d))
    to_right.start()
    to_left.start()
    for d in order:
        sends[d - 1].start()

    def forward(d, source):
        column = lax.rem(me + src_count - d, src_count)
        return pltpu.make_async_remote_copy(
            src_ref=source(column), dst_ref=buf.at[column, landing], send_sem=halo_send.at[d],
            recv_sem=halo_recv.at[d], device_id={"tgt": 1 - half}, device_id_type=MESH,
        )

    forwards = []
    if tgt_count > 1:
        offset = pl.multiple_of((1 - half) * (rows - HALO), HALO)
        forwards.append(forward(0, lambda column: tgt_hbm.at[pl.ds(offset, HALO)]))
        forwards[0].start()

    zero_block = jnp.zeros((span, width), BF16)
    for ref in (vol, sec):
        ref[pl.ds(0, span), :] = zero_block
        ref[pl.ds((breadth + 1) * span, span), :] = zero_block
    for copy in own[2:5]:
        copy.wait()
    expand = (iota((groups, width), 1) % groups == iota((groups, width), 0)).astype(BF16)
    spread = [dot(taps[i], expand).astype(BF16) for i in range(3)]
    lane_group = iota((groups, width), 1) // groups
    nothing = jnp.zeros((groups, width), BF16)

    def tap(i, a, b):
        start = (a * 3 + b) * groups
        return spread[i][start : start + groups]

    for a in range(3):
        for b in range(3):
            for j in range(width // groups):
                w1[a, pl.ds(b * width + j * groups, groups), :] = jnp.where(
                    lane_group == j, tap(0, a, b), nothing
                )
    for j in range(width // groups):
        k, h = divmod(j, window_rows)
        two = nothing
        three = [nothing[:, :LANES]] * 3
        if k < 3:
            for a in range(3):
                two = jnp.where(lane_group % window_rows == h - a + 1, tap(1, a, k), two)
                three[a] = jnp.where(
                    (lane_group % window_rows == h)[:, :LANES], tap(2, a, k)[:, :LANES], three[a]
                )
        w2[pl.ds(j * groups, groups), :] = two
        for a in range(3):
            w3[pl.ds(j * groups, groups), pl.ds(a * LANES, LANES)] = three[a]

    def valid(extra):
        position = iota((chunk_rows, width), 0) % span
        low = half * (HALO - extra)
        return (position >= low) & (position < low + rows + extra)

    own[1].wait()
    own[5].wait()
    own[6].wait()
    to_right.wait()
    to_left.wait()
    row_of = iota((column_lanes, map_rows), 0) // groups
    wanted = jnp.zeros((column_lanes, map_rows), jnp.int32)
    for h in range(window_rows):
        wanted = jnp.where(row_of == h, rows_ref[h], wanted)
    select = (iota((column_lanes, map_rows), 1) == wanted).astype(BF16)
    same_group = (
        iota((column_lanes, features), 1) // channels == iota((column_lanes, features), 0) % groups
    )
    parts = []
    for k in range(3):
        keep = same_group
        if k == 0:
            keep = keep & (me > 0)
        if k == 2:
            keep = keep & (me < src_count - 1)
        parts.append(jnp.where(keep, dot(select, sbuf[k]), 0.0).astype(BF16))
    if width > 3 * column_lanes:
        parts.append(jnp.zeros((width - 3 * column_lanes, features), BF16))
    weights = jnp.concatenate(parts, axis=0)

    own[0].wait()
    for d in range(1, src_count):
        sends[d - 1].wait_recv()
        if tgt_count > 1:
            copy = forward(d, lambda column: buf.at[column, edge])
            copy.start()
            forwards.append(copy)
    for copy in forwards:
        copy.wait_recv()

    def volume_chunk(chunk):
        window = jnp.concatenate(
            [buf[cols_ref[chunk * per_block + i]] for i in range(per_block)], axis=0
        )
        scores = lax.dot_general(
            window, weights, (((1,), (1,)), ((), ())), preferred_element_type=F32
        ) * (channels ** -0.5)
        vol[pl.ds(pl.multiple_of((chunk * per_block + 1) * span, span), chunk_rows), :] = (
            jnp.where(valid(2), scores, 0.0).astype(BF16)
        )

    def at(chunk, b):
        return pl.ds(pl.multiple_of((chunk * per_block + b) * span, span), chunk_rows)

    def shifted(parts):
        total = parts[1] + pltpu.roll(parts[0], 1, 0)
        return total + pltpu.roll(parts[2], chunk_rows - 1, 0)

    def middle_chunk(chunk):
        window = jnp.concatenate([vol[at(chunk, b), :] for b in range(3)], axis=1)
        one = shifted([dot(window, w1[a]) for a in range(3)])
        one = jnp.maximum(one, 0.0).astype(BF16)
        two = jnp.maximum(dot(one, w2[...]), 0.0)
        sec[at(chunk, 1), :] = jnp.where(valid(1), two, 0.0).astype(BF16)

    def last_chunk(chunk):
        which = iota((chunk_rows, width), 1) // column_lanes
        window = jnp.where(
            which == 0,
            sec[at(chunk, 0), :],
            jnp.where(which == 1, sec[at(chunk, 1), :], sec[at(chunk, 2), :]),
        )
        three = dot(window, w3[...])
        three = shifted([three[:, a * LANES : (a + 1) * LANES] for a in range(3)])
        stage[...] = jnp.maximum(three, 0.0)
        pieces = [
            stage[pl.ds(pl.multiple_of(i * span + half * HALO, HALO), rows), :]
            for i in range(per_block)
        ]
        group = iota((rows, LANES), 1) // groups
        rolled = []
        for d in range(window_rows):
            mixed = pieces[d % per_block]
            for j in range(1, per_block):
                mixed = jnp.where(group == j, pieces[(j + d) % per_block], mixed)
            rolled.append(pltpu.roll(mixed, d * groups, 1) if d else mixed)
        for h in range(window_rows):
            total = rolled[0]
            for d in range(1, window_rows):
                total = jnp.where((group - h) % window_rows == d, rolled[d], total)
            out_ref[h, :, pl.ds(pl.multiple_of(chunk * LANES, LANES), LANES)] = total.astype(BF16)

    for step in (volume_chunk, middle_chunk, last_chunk):
        if chunks == 1:
            step(0)
        else:
            pl.loop(0, chunks)(step)

    for copy in sends:
        copy.wait_send()
    for copy in forwards:
        copy.wait_send()


def local(
    src_count,
    tgt_count,
    source_features,
    target_features,
    source_rows,
    target_cols,
    target_kernel_one,
    source_kernel,
    target_kernel_two,
):
    groups = source_kernel.shape[2]
    window_rows = source_rows.shape[0]
    breadth = target_cols.shape[0]
    map_rows, _, features = source_features.shape
    rows = target_features.shape[0]
    span = rows + HALO
    width = -(-3 * window_rows * groups // LANES) * LANES
    chunk_rows = LANES // groups * span
    taps = 9 * groups
    hbm = pl.BlockSpec(memory_space=pltpu.HBM)
    dma = pltpu.SemaphoreType.DMA
    out = pl.pallas_call(
        functools.partial(kernel, src_count, tgt_count, breadth, window_rows, groups),
        out_shape=jax.ShapeDtypeStruct((window_rows, rows, breadth * groups), BF16),
        in_specs=[hbm] * 7,
        out_specs=pl.BlockSpec(memory_space=pltpu.VMEM),
        scratch_shapes=[
            pltpu.SMEM((window_rows,), jnp.int32),
            pltpu.SMEM((breadth,), jnp.int32),
            pltpu.VMEM((breadth, span, features), BF16),
            pltpu.VMEM((3, map_rows, features), BF16),
            pltpu.VMEM((3, taps, groups), BF16),
            pltpu.VMEM(((breadth + 2) * span, width), BF16),
            pltpu.VMEM(((breadth + 2) * span, width), BF16),
            pltpu.VMEM((chunk_rows, LANES), F32),
            pltpu.VMEM((3, 3 * width, width), BF16),
            pltpu.VMEM((width, width), BF16),
            pltpu.VMEM((width, 3 * LANES), BF16),
            dma((7,)),
            dma((src_count,)),
            dma((src_count,)),
            dma((src_count,)),
            dma((src_count,)),
            dma((2,)),
            dma((2,)),
        ],
        compiler_params=pltpu.CompilerParams(
            collective_id=0, has_side_effects=True, vmem_limit_bytes=64 * 1024 * 1024
        ),
    )(
        source_rows,
        target_cols,
        target_features[:, 0],
        source_features[:, 0],
        target_kernel_one.reshape(taps, groups),
        source_kernel.reshape(taps, groups),
        target_kernel_two.reshape(taps, groups),
    )
    return out[:, None]


def solution(mesh):
    return jax.shard_map(
        functools.partial(local, mesh.shape["src"], mesh.shape["tgt"]),
        mesh=mesh,
        in_specs=(
            P("pair", "src", None),
            P(("pair", "tgt"), "src", None),
            P("pair"),
            P("pair"),
            P(),
            P(),
            P(),
        ),
        out_specs=P("pair", "src", "tgt", None),
        check_vma=False,
    )
```

```python
import functools

import jax
import jax.numpy as jnp
from jax import lax
from jax.experimental import pallas as pl
from jax.experimental.pallas import tpu as pltpu
from jax.sharding import PartitionSpec as P

MESH = pl.DeviceIdType.MESH
LANES = 128
HALO = 16
BF16 = jnp.bfloat16
F32 = jnp.float32


def iota(shape, dim):
    return lax.broadcasted_iota(jnp.int32, shape, dim)


def dot(a, b):
    return jnp.dot(a, b, preferred_element_type=F32)


def kernel(
    src_count,
    tgt_count,
    breadth,
    window_rows,
    groups,
    rows_hbm,
    cols_hbm,
    tgt_hbm,
    src_hbm,
    k1_hbm,
    ks_hbm,
    k2_hbm,
    out_ref,
    rows_ref,
    cols_ref,
    buf,
    sbuf,
    taps,
    vol,
    sec,
    stage,
    w1,
    w2,
    w3,
    local_sem,
    send_sem,
    recv_sem,
    halo_send,
    halo_recv,
    src_send,
    src_recv,
):
    rows, features = tgt_hbm.shape
    map_rows = src_hbm.shape[0]
    channels = features // groups
    span = rows + HALO
    width = vol.shape[1]
    column_lanes = window_rows * groups
    per_block = LANES // groups
    chunks = breadth // per_block
    chunk_rows = per_block * span
    me = lax.axis_index("src")
    half = lax.axis_index("tgt")
    main = pl.ds(pl.multiple_of(half * HALO, HALO), rows)

    def peer(d):
        return lax.rem(me + d, src_count)

    barrier = pltpu.get_barrier_semaphore()
    for d in range(1, src_count):
        pl.semaphore_signal(barrier, inc=1, device_id={"src": peer(d)}, device_id_type=MESH)
    if tgt_count > 1:
        pl.semaphore_signal(barrier, inc=1, device_id={"tgt": 1 - half}, device_id_type=MESH)

    own = [
        pltpu.make_async_copy(tgt_hbm, buf.at[me, main], local_sem.at[0]),
        pltpu.make_async_copy(src_hbm, sbuf.at[1], local_sem.at[1]),
        pltpu.make_async_copy(k1_hbm, taps.at[0], local_sem.at[2]),
        pltpu.make_async_copy(ks_hbm, taps.at[1], local_sem.at[3]),
        pltpu.make_async_copy(k2_hbm, taps.at[2], local_sem.at[4]),
        pltpu.make_async_copy(rows_hbm, rows_ref, local_sem.at[5]),
        pltpu.make_async_copy(cols_hbm, cols_ref, local_sem.at[6]),
    ]
    for copy in own:
        copy.start()
    pl.semaphore_wait(barrier, src_count - 1 + (1 if tgt_count > 1 else 0))

    edge = pl.ds(pl.multiple_of(half * HALO + (1 - half) * (rows - HALO), HALO), HALO)
    landing = pl.ds(pl.multiple_of(half * rows, HALO), HALO)

    to_right = pltpu.make_async_remote_copy(
        src_ref=src_hbm, dst_ref=sbuf.at[0], send_sem=src_send.at[0], recv_sem=src_recv.at[0],
        device_id={"src": lax.rem(me + 1, src_count)}, device_id_type=MESH,
    )
    to_left = pltpu.make_async_remote_copy(
        src_ref=src_hbm, dst_ref=sbuf.at[2], send_sem=src_send.at[1], recv_sem=src_recv.at[1],
        device_id={"src": lax.rem(me + src_count - 1, src_count)}, device_id_type=MESH,
    )
    sends = []
    for d in range(1, src_count):
        sends.append(
            pltpu.make_async_remote_copy(
                src_ref=tgt_hbm, dst_ref=buf.at[me, main], send_sem=send_sem.at[d],
                recv_sem=recv_sem.at[d], device_id={"src": peer(d)}, device_id_type=MESH,
            )
        )
    order = sorted(range(1, src_count), key=lambda d: -min(d, src_count - d))
    to_right.start()
    to_left.start()
    for d in order:
        sends[d - 1].start()

    def forward(d, source):
        column = lax.rem(me + src_count - d, src_count)
        return pltpu.make_async_remote_copy(
            src_ref=source(column), dst_ref=buf.at[column, landing], send_sem=halo_send.at[d],
            recv_sem=halo_recv.at[d], device_id={"tgt": 1 - half}, device_id_type=MESH,
        )

    forwards = []
    if tgt_count > 1:
        offset = pl.multiple_of((1 - half) * (rows - HALO), HALO)
        forwards.append(forward(0, lambda column: tgt_hbm.at[pl.ds(offset, HALO)]))
        forwards[0].start()

    zero_block = jnp.zeros((span, width), BF16)
    for ref in (vol, sec):
        ref[pl.ds(0, span), :] = zero_block
        ref[pl.ds((breadth + 1) * span, span), :] = zero_block
    for copy in own[2:5]:
        copy.wait()
    expand = (iota((groups, width), 1) % groups == iota((groups, width), 0)).astype(BF16)
    spread = [dot(taps[i], expand).astype(BF16) for i in range(3)]
    lane_group = iota((groups, width), 1) // groups
    nothing = jnp.zeros((groups, width), BF16)

    def tap(i, a, b):
        start = (a * 3 + b) * groups
        return spread[i][start : start + groups]

    for a in range(3):
        for b in range(3):
            for j in range(width // groups):
                w1[a, pl.ds(b * width + j * groups, groups), :] = jnp.where(
                    lane_group == j, tap(0, a, b), nothing
                )
    for j in range(width // groups):
        k, h = divmod(j, window_rows)
        two = nothing
        three = [nothing[:, :LANES]] * 3
        if k < 3:
            for a in range(3):
                two = jnp.where(lane_group % window_rows == h - a + 1, tap(1, a, k), two)
                three[a] = jnp.where(
                    (lane_group % window_rows == h)[:, :LANES], tap(2, a, k)[:, :LANES], three[a]
                )
        w2[pl.ds(j * groups, groups), :] = two
        for a in range(3):
            w3[pl.ds(j * groups, groups), pl.ds(a * LANES, LANES)] = three[a]

    def valid(extra):
        position = iota((chunk_rows, width), 0) % span
        low = half * (HALO - extra)
        return (position >= low) & (position < low + rows + extra)

    own[1].wait()
    own[5].wait()
    own[6].wait()
    to_right.wait()
    to_left.wait()
    row_of = iota((column_lanes, map_rows), 0) // groups
    wanted = jnp.zeros((column_lanes, map_rows), jnp.int32)
    for h in range(window_rows):
        wanted = jnp.where(row_of == h, rows_ref[h], wanted)
    select = (iota((column_lanes, map_rows), 1) == wanted).astype(BF16)
    same_group = (
        iota((column_lanes, features), 1) // channels == iota((column_lanes, features), 0) % groups
    )
    parts = []
    for k in range(3):
        keep = same_group
        if k == 0:
            keep = keep & (me > 0)
        if k == 2:
            keep = keep & (me < src_count - 1)
        parts.append(jnp.where(keep, dot(select, sbuf[k]), 0.0).astype(BF16))
    if width > 3 * column_lanes:
        parts.append(jnp.zeros((width - 3 * column_lanes, features), BF16))
    weights = jnp.concatenate(parts, axis=0)

    own[0].wait()
    for d in range(1, src_count):
        sends[d - 1].wait_recv()
        if tgt_count > 1:
            copy = forward(d, lambda column: buf.at[column, edge])
            copy.start()
            forwards.append(copy)
    for copy in forwards:
        copy.wait_recv()

    def volume_chunk(chunk):
        window = jnp.concatenate(
            [buf[cols_ref[chunk * per_block + i]] for i in range(per_block)], axis=0
        )
        scores = lax.dot_general(
            window, weights, (((1,), (1,)), ((), ())), preferred_element_type=F32
        ) * (channels ** -0.5)
        vol[pl.ds(pl.multiple_of((chunk * per_block + 1) * span, span), chunk_rows), :] = (
            jnp.where(valid(2), scores, 0.0).astype(BF16)
        )

    def at(chunk, b):
        return pl.ds(pl.multiple_of((chunk * per_block + b) * span, span), chunk_rows)

    def shifted(parts):
        total = parts[1] + pltpu.roll(parts[0], 1, 0)
        return total + pltpu.roll(parts[2], chunk_rows - 1, 0)

    def middle_chunk(chunk):
        window = jnp.concatenate([vol[at(chunk, b), :] for b in range(3)], axis=1)
        one = shifted([dot(window, w1[a]) for a in range(3)])
        one = jnp.maximum(one, 0.0).astype(BF16)
        two = jnp.maximum(dot(one, w2[...]), 0.0)
        sec[at(chunk, 1), :] = jnp.where(valid(1), two, 0.0).astype(BF16)

    def last_chunk(chunk):
        which = iota((chunk_rows, width), 1) // column_lanes
        window = jnp.where(
            which == 0,
            sec[at(chunk, 0), :],
            jnp.where(which == 1, sec[at(chunk, 1), :], sec[at(chunk, 2), :]),
        )
        three = dot(window, w3[...])
        three = shifted([three[:, a * LANES : (a + 1) * LANES] for a in range(3)])
        stage[...] = jnp.maximum(three, 0.0)
        pieces = [
            stage[pl.ds(pl.multiple_of(i * span + half * HALO, HALO), rows), :]
            for i in range(per_block)
        ]
        group = iota((rows, LANES), 1) // groups
        rolled = []
        for d in range(window_rows):
            mixed = pieces[d % per_block]
            for j in range(1, per_block):
                mixed = jnp.where(group == j, pieces[(j + d) % per_block], mixed)
            rolled.append(pltpu.roll(mixed, d * groups, 1) if d else mixed)
        for h in range(window_rows):
            total = rolled[0]
            for d in range(1, window_rows):
                total = jnp.where((group - h) % window_rows == d, rolled[d], total)
            out_ref[h, :, pl.ds(pl.multiple_of(chunk * LANES, LANES), LANES)] = total.astype(BF16)

    for step in (volume_chunk, middle_chunk, last_chunk):
        if chunks == 1:
            step(0)
        else:
            pl.loop(0, chunks)(step)

    for copy in sends:
        copy.wait_send()
    for copy in forwards:
        copy.wait_send()


def local(
    src_count,
    tgt_count,
    source_features,
    target_features,
    source_rows,
    target_cols,
    target_kernel_one,
    source_kernel,
    target_kernel_two,
):
    groups = source_kernel.shape[2]
    window_rows = source_rows.shape[0]
    breadth = target_cols.shape[0]
    map_rows, _, features = source_features.shape
    rows = target_features.shape[0]
    span = rows + HALO
    width = -(-3 * window_rows * groups // LANES) * LANES
    chunk_rows = LANES // groups * span
    taps = 9 * groups
    hbm = pl.BlockSpec(memory_space=pltpu.HBM)
    operands = (
        source_rows,
        target_cols,
        target_features[:, 0],
        source_features[:, 0],
        target_kernel_one.reshape(taps, groups),
        source_kernel.reshape(taps, groups),
        target_kernel_two.reshape(taps, groups),
    )
    dma = pltpu.SemaphoreType.DMA
    out = pl.pallas_call(
        functools.partial(kernel, src_count, tgt_count, breadth, window_rows, groups),
        out_shape=jax.ShapeDtypeStruct((window_rows, rows, breadth * groups), BF16),
        in_specs=[hbm] * 7,
        out_specs=pl.BlockSpec(memory_space=pltpu.VMEM),
        scratch_shapes=[
            pltpu.SMEM((window_rows,), jnp.int32),
            pltpu.SMEM((breadth,), jnp.int32),
            pltpu.VMEM((breadth, span, features), BF16),
            pltpu.VMEM((3, map_rows, features), BF16),
            pltpu.VMEM((3, taps, groups), BF16),
            pltpu.VMEM(((breadth + 2) * span, width), BF16),
            pltpu.VMEM(((breadth + 2) * span, width), BF16),
            pltpu.VMEM((chunk_rows, LANES), F32),
            pltpu.VMEM((3, 3 * width, width), BF16),
            pltpu.VMEM((width, width), BF16),
            pltpu.VMEM((width, 3 * LANES), BF16),
            dma((7,)),
            dma((src_count,)),
            dma((src_count,)),
            dma((src_count,)),
            dma((src_count,)),
            dma((2,)),
            dma((2,)),
        ],
        compiler_params=pltpu.CompilerParams(
            collective_id=0, has_side_effects=True, vmem_limit_bytes=48 * 1024 * 1024
        ),
    )(*(pltpu.with_memory_space_constraint(operand, pltpu.HBM) for operand in operands))
    return out[:, None]


def solution(mesh):
    return jax.shard_map(
        functools.partial(local, mesh.shape["src"], mesh.shape["tgt"]),
        mesh=mesh,
        in_specs=(
            P("pair", "src", None),
            P(("pair", "tgt"), "src", None),
            P("pair"),
            P("pair"),
            P(),
            P(),
            P(),
        ),
        out_specs=P("pair", "src", "tgt", None),
        check_vma=False,
    )
```

```python
import functools

import jax
import jax.numpy as jnp
from jax import lax
from jax.experimental import pallas as pl
from jax.experimental.pallas import tpu as pltpu
from jax.sharding import PartitionSpec as P

MESH = pl.DeviceIdType.MESH
LANES = 128
HALO = 16
BF16 = jnp.bfloat16
F32 = jnp.float32


def iota(shape, dim):
    return lax.broadcasted_iota(jnp.int32, shape, dim)


def dot(a, b):
    return jnp.dot(a, b, preferred_element_type=F32)


def kernel(
    src_count,
    tgt_count,
    breadth,
    window_rows,
    groups,
    rows_hbm,
    cols_hbm,
    tgt_hbm,
    src_hbm,
    k1_hbm,
    ks_hbm,
    k2_hbm,
    out_ref,
    rows_ref,
    cols_ref,
    buf,
    sbuf,
    taps,
    vol,
    rim,
    edges,
    acc,
    sec,
    stage,
    w1,
    w2,
    w3,
    local_sem,
    send_sem,
    recv_sem,
    halo_send,
    halo_recv,
    src_send,
    src_recv,
):
    rows, features = tgt_hbm.shape
    map_rows = src_hbm.shape[0]
    channels = features // groups
    span = rows + HALO
    width = vol.shape[2]
    column_lanes = window_rows * groups
    per_block = LANES // groups
    chunks = breadth // per_block
    chunk_rows = per_block * span
    me = lax.axis_index("src")
    half = lax.axis_index("tgt")
    main = pl.ds(pl.multiple_of(half * HALO, HALO), rows)

    def peer(d):
        return lax.rem(me + d, src_count)

    barrier = pltpu.get_barrier_semaphore()
    for d in range(1, src_count):
        pl.semaphore_signal(barrier, inc=1, device_id={"src": peer(d)}, device_id_type=MESH)
    if tgt_count > 1:
        pl.semaphore_signal(barrier, inc=1, device_id={"tgt": 1 - half}, device_id_type=MESH)

    own = [
        pltpu.make_async_copy(tgt_hbm, buf.at[me], local_sem.at[0]),
        pltpu.make_async_copy(src_hbm, sbuf.at[1], local_sem.at[1]),
        pltpu.make_async_copy(k1_hbm, taps.at[0], local_sem.at[2]),
        pltpu.make_async_copy(ks_hbm, taps.at[1], local_sem.at[3]),
        pltpu.make_async_copy(k2_hbm, taps.at[2], local_sem.at[4]),
        pltpu.make_async_copy(rows_hbm, rows_ref, local_sem.at[5]),
        pltpu.make_async_copy(cols_hbm, cols_ref, local_sem.at[6]),
    ]
    for copy in own:
        copy.start()
    pl.semaphore_wait(barrier, src_count - 1 + (1 if tgt_count > 1 else 0))

    edge = pl.ds(pl.multiple_of((1 - half) * (rows - HALO), HALO), HALO)
    arrived = pl.ds(pl.multiple_of((1 - half) * rows, HALO), HALO)

    to_right = pltpu.make_async_remote_copy(
        src_ref=src_hbm, dst_ref=sbuf.at[0], send_sem=src_send.at[0], recv_sem=src_recv.at[0],
        device_id={"src": lax.rem(me + 1, src_count)}, device_id_type=MESH,
    )
    to_left = pltpu.make_async_remote_copy(
        src_ref=src_hbm, dst_ref=sbuf.at[2], send_sem=src_send.at[1], recv_sem=src_recv.at[1],
        device_id={"src": lax.rem(me + src_count - 1, src_count)}, device_id_type=MESH,
    )
    sends = []
    for d in range(1, src_count):
        sends.append(
            pltpu.make_async_remote_copy(
                src_ref=tgt_hbm, dst_ref=buf.at[me], send_sem=send_sem.at[d],
                recv_sem=recv_sem.at[d], device_id={"src": peer(d)}, device_id_type=MESH,
            )
        )
    order = sorted(range(1, src_count), key=lambda d: -min(d, src_count - d))
    to_right.start()
    to_left.start()
    for d in order:
        sends[d - 1].start()

    exchange = pltpu.make_async_remote_copy(
        src_ref=edges, dst_ref=rim.at[pl.ds(0, breadth)], send_sem=halo_send.at[0],
        recv_sem=halo_recv.at[0], device_id={"tgt": 1 - half}, device_id_type=MESH,
    )

    zero_block = jnp.zeros((span, width), BF16)
    vol[breadth] = zero_block[:rows]
    rim[breadth] = zero_block[:HALO]
    if tgt_count == 1:
        for column in range(breadth):
            rim[column] = zero_block[:HALO]
    sec[pl.ds(0, span), :] = zero_block
    sec[pl.ds((breadth + 1) * span, span), :] = zero_block
    for copy in own[2:5]:
        copy.wait()
    expand = (iota((groups, width), 1) % groups == iota((groups, width), 0)).astype(BF16)
    spread = [dot(taps[i], expand).astype(BF16) for i in range(3)]
    lane_group = iota((groups, width), 1) // groups
    nothing = jnp.zeros((groups, width), BF16)

    def tap(i, a, b):
        start = (a * 3 + b) * groups
        return spread[i][start : start + groups]

    for a in range(3):
        for b in range(3):
            for j in range(width // groups):
                w1[a, pl.ds(b * width + j * groups, groups), :] = jnp.where(
                    lane_group == j, tap(0, a, b), nothing
                )
    for j in range(width // groups):
        k, h = divmod(j, window_rows)
        two = nothing
        three = [nothing[:, :LANES]] * 3
        if k < 3:
            for a in range(3):
                two = jnp.where(lane_group % window_rows == h - a + 1, tap(1, a, k), two)
                three[a] = jnp.where(
                    (lane_group % window_rows == h)[:, :LANES], tap(2, a, k)[:, :LANES], three[a]
                )
        w2[pl.ds(j * groups, groups), :] = two
        for a in range(3):
            w3[pl.ds(j * groups, groups), pl.ds(a * LANES, LANES)] = three[a]

    def valid(extra):
        position = iota((chunk_rows, width), 0) % span
        low = half * (HALO - extra)
        return (position >= low) & (position < low + rows + extra)

    own[1].wait()
    own[5].wait()
    own[6].wait()
    to_right.wait()
    to_left.wait()
    row_of = iota((column_lanes, map_rows), 0) // groups
    wanted = jnp.zeros((column_lanes, map_rows), jnp.int32)
    for h in range(window_rows):
        wanted = jnp.where(row_of == h, rows_ref[h], wanted)
    select = (iota((column_lanes, map_rows), 1) == wanted).astype(BF16)
    same_group = (
        iota((column_lanes, features), 1) // channels == iota((column_lanes, features), 0) % groups
    )
    parts = []
    for k in range(3):
        keep = same_group
        if k == 0:
            keep = keep & (me > 0)
        if k == 2:
            keep = keep & (me < src_count - 1)
        parts.append(jnp.where(keep, dot(select, sbuf[k]), 0.0).astype(BF16))
    if width > 3 * column_lanes:
        parts.append(jnp.zeros((width - 3 * column_lanes, features), BF16))
    weights = jnp.concatenate(parts, axis=0)

    position = iota((HALO, width), 0)
    first_kept = (1 - half) * (HALO - 2)
    kept = (position >= first_kept) & (position < first_kept + 2)

    def score(column):
        scores = lax.dot_general(
            buf[column], weights, (((1,), (1,)), ((), ())), preferred_element_type=F32
        ) * (channels ** -0.5)
        vol[column] = scores.astype(BF16)
        if tgt_count > 1:
            edges[column] = jnp.where(kept, vol[column, edge, :], zero_block[:HALO])

    own[0].wait()
    score(me)
    for d in reversed(order):
        sends[d - 1].wait_recv()
        score(lax.rem(me + src_count - d, src_count))
    if tgt_count > 1:
        exchange.start()

    def gather(chunk, held):
        taps_of_row = []
        for b in range(3):
            blocks = []
            for i in range(per_block):
                spot = chunk * per_block + i + b - 1
                inside = (spot >= 0) & (spot < breadth)
                known = cols_ref[jnp.clip(spot, 0, breadth - 1)]
                blocks.append(held[jnp.where(inside, known, breadth)])
            taps_of_row.append(jnp.concatenate(blocks, axis=0))
        return jnp.concatenate(taps_of_row, axis=1)

    def first_part(chunk, held, place):
        window = gather(chunk, held)
        home = pl.ds(pl.multiple_of(chunk * per_block, per_block), per_block)
        for a in range(3):
            acc[a, home, place, :] = dot(window, w1[a]).reshape(per_block, -1, width)

    def main_chunk(chunk):
        first_part(chunk, vol, main)

    def at(chunk, b):
        return pl.ds(pl.multiple_of((chunk * per_block + b) * span, span), chunk_rows)

    def shifted(parts):
        total = parts[1] + pltpu.roll(parts[0], 1, 0)
        return total + pltpu.roll(parts[2], chunk_rows - 1, 0)

    def middle_chunk(chunk):
        first_part(chunk, rim, arrived)
        home = pl.ds(pl.multiple_of(chunk * per_block, per_block), per_block)
        one = shifted([acc[a, home].reshape(chunk_rows, width) for a in range(3)])
        one = jnp.maximum(one, 0.0).astype(BF16)
        two = jnp.maximum(dot(one, w2[...]), 0.0)
        sec[at(chunk, 1), :] = jnp.where(valid(1), two, 0.0).astype(BF16)

    def last_chunk(chunk):
        which = iota((chunk_rows, width), 1) // column_lanes
        window = jnp.where(
            which == 0,
            sec[at(chunk, 0), :],
            jnp.where(which == 1, sec[at(chunk, 1), :], sec[at(chunk, 2), :]),
        )
        three = dot(window, w3[...])
        three = shifted([three[:, a * LANES : (a + 1) * LANES] for a in range(3)])
        stage[...] = jnp.maximum(three, 0.0)
        pieces = [
            stage[pl.ds(pl.multiple_of(i * span + half * HALO, HALO), rows), :]
            for i in range(per_block)
        ]
        group = iota((rows, LANES), 1) // groups
        rolled = []
        for d in range(window_rows):
            mixed = pieces[d % per_block]
            for j in range(1, per_block):
                mixed = jnp.where(group == j, pieces[(j + d) % per_block], mixed)
            rolled.append(pltpu.roll(mixed, d * groups, 1) if d else mixed)
        for h in range(window_rows):
            total = rolled[0]
            for d in range(1, window_rows):
                total = jnp.where((group - h) % window_rows == d, rolled[d], total)
            out_ref[h, :, pl.ds(pl.multiple_of(chunk * LANES, LANES), LANES)] = total.astype(BF16)

    for step in (main_chunk, middle_chunk, last_chunk):
        if step is middle_chunk and tgt_count > 1:
            exchange.wait_recv()
        if chunks == 1:
            step(0)
        else:
            pl.loop(0, chunks)(step)

    for copy in sends:
        copy.wait_send()
    if tgt_count > 1:
        exchange.wait_send()


def local(
    src_count,
    tgt_count,
    source_features,
    target_features,
    source_rows,
    target_cols,
    target_kernel_one,
    source_kernel,
    target_kernel_two,
):
    groups = source_kernel.shape[2]
    window_rows = source_rows.shape[0]
    breadth = target_cols.shape[0]
    map_rows, _, features = source_features.shape
    rows = target_features.shape[0]
    span = rows + HALO
    width = -(-3 * window_rows * groups // LANES) * LANES
    chunk_rows = LANES // groups * span
    taps = 9 * groups
    hbm = pl.BlockSpec(memory_space=pltpu.HBM)
    operands = (
        source_rows,
        target_cols,
        target_features[:, 0],
        source_features[:, 0],
        target_kernel_one.reshape(taps, groups),
        source_kernel.reshape(taps, groups),
        target_kernel_two.reshape(taps, groups),
    )
    dma = pltpu.SemaphoreType.DMA
    out = pl.pallas_call(
        functools.partial(kernel, src_count, tgt_count, breadth, window_rows, groups),
        out_shape=jax.ShapeDtypeStruct((window_rows, rows, breadth * groups), BF16),
        in_specs=[hbm] * 7,
        out_specs=pl.BlockSpec(memory_space=pltpu.VMEM),
        scratch_shapes=[
            pltpu.SMEM((window_rows,), jnp.int32),
            pltpu.SMEM((breadth,), jnp.int32),
            pltpu.VMEM((breadth, rows, features), BF16),
            pltpu.VMEM((3, map_rows, features), BF16),
            pltpu.VMEM((3, taps, groups), BF16),
            pltpu.VMEM((breadth + 1, rows, width), BF16),
            pltpu.VMEM((breadth + 1, HALO, width), BF16),
            pltpu.VMEM((breadth, HALO, width), BF16),
            pltpu.VMEM((3, breadth, span, width), F32),
            pltpu.VMEM(((breadth + 2) * span, width), BF16),
            pltpu.VMEM((chunk_rows, LANES), F32),
            pltpu.VMEM((3, 3 * width, width), BF16),
            pltpu.VMEM((width, width), BF16),
            pltpu.VMEM((width, 3 * LANES), BF16),
            dma((7,)),
            dma((src_count,)),
            dma((src_count,)),
            dma((1,)),
            dma((1,)),
            dma((2,)),
            dma((2,)),
        ],
        compiler_params=pltpu.CompilerParams(
            collective_id=0, has_side_effects=True, vmem_limit_bytes=48 * 1024 * 1024
        ),
    )(*(pltpu.with_memory_space_constraint(operand, pltpu.HBM) for operand in operands))
    return out[:, None]


def solution(mesh):
    return jax.shard_map(
        functools.partial(local, mesh.shape["src"], mesh.shape["tgt"]),
        mesh=mesh,
        in_specs=(
            P("pair", "src", None),
            P(("pair", "tgt"), "src", None),
            P("pair"),
            P("pair"),
            P(),
            P(),
            P(),
        ),
        out_specs=P("pair", "src", "tgt", None),
        check_vma=False,
    )
```

```python
import functools

import jax
import jax.numpy as jnp
from jax import lax
from jax.experimental import pallas as pl
from jax.experimental.pallas import tpu as pltpu
from jax.sharding import PartitionSpec as P

MESH = pl.DeviceIdType.MESH
LANES = 128
HALO = 16
BF16 = jnp.bfloat16
F32 = jnp.float32


def iota(shape, dim):
    return lax.broadcasted_iota(jnp.int32, shape, dim)


def quotient(x, n):
    return x >> (n.bit_length() - 1) if n & (n - 1) == 0 else x // n


def remainder(x, n):
    return x & (n - 1) if n & (n - 1) == 0 else x % n


def dot(a, b):
    return jnp.dot(a, b, preferred_element_type=F32)


def kernel(
    src_count,
    tgt_count,
    breadth,
    window_rows,
    groups,
    rows_hbm,
    cols_hbm,
    tgt_hbm,
    src_hbm,
    k1_hbm,
    ks_hbm,
    k2_hbm,
    out_ref,
    rows_ref,
    cols_ref,
    buf,
    sbuf,
    taps,
    vol,
    sec,
    stage,
    w1,
    w2,
    w3,
    local_sem,
    send_sem,
    recv_sem,
    halo_send,
    halo_recv,
    src_send,
    src_recv,
):
    rows, features = tgt_hbm.shape
    map_rows = src_hbm.shape[0]
    channels = features // groups
    span = rows + HALO
    width = vol.shape[2]
    column_lanes = window_rows * groups
    per_block = LANES // groups
    chunks = breadth // per_block
    chunk_rows = per_block * span
    me = lax.axis_index("src")
    half = lax.axis_index("tgt")
    main = pl.ds(pl.multiple_of(half * HALO, HALO), rows)

    def peer(d):
        return lax.rem(me + d, src_count)

    barrier = pltpu.get_barrier_semaphore()
    for d in range(1, src_count):
        pl.semaphore_signal(barrier, inc=1, device_id={"src": peer(d)}, device_id_type=MESH)
    if tgt_count > 1:
        pl.semaphore_signal(barrier, inc=1, device_id={"tgt": 1 - half}, device_id_type=MESH)

    own = [
        pltpu.make_async_copy(tgt_hbm, buf.at[me, main], local_sem.at[0]),
        pltpu.make_async_copy(src_hbm, sbuf.at[1], local_sem.at[1]),
        pltpu.make_async_copy(k1_hbm, taps.at[0], local_sem.at[2]),
        pltpu.make_async_copy(ks_hbm, taps.at[1], local_sem.at[3]),
        pltpu.make_async_copy(k2_hbm, taps.at[2], local_sem.at[4]),
        pltpu.make_async_copy(rows_hbm, rows_ref, local_sem.at[5]),
        pltpu.make_async_copy(cols_hbm, cols_ref, local_sem.at[6]),
    ]
    for copy in own:
        copy.start()
    pl.semaphore_wait(barrier, src_count - 1 + (1 if tgt_count > 1 else 0))

    edge = pl.ds(pl.multiple_of(half * HALO + (1 - half) * (rows - HALO), HALO), HALO)
    landing = pl.ds(pl.multiple_of(half * rows, HALO), HALO)

    to_right = pltpu.make_async_remote_copy(
        src_ref=src_hbm, dst_ref=sbuf.at[0], send_sem=src_send.at[0], recv_sem=src_recv.at[0],
        device_id={"src": lax.rem(me + 1, src_count)}, device_id_type=MESH,
    )
    to_left = pltpu.make_async_remote_copy(
        src_ref=src_hbm, dst_ref=sbuf.at[2], send_sem=src_send.at[1], recv_sem=src_recv.at[1],
        device_id={"src": lax.rem(me + src_count - 1, src_count)}, device_id_type=MESH,
    )
    sends = []
    for d in range(1, src_count):
        sends.append(
            pltpu.make_async_remote_copy(
                src_ref=tgt_hbm, dst_ref=buf.at[me, main], send_sem=send_sem.at[d],
                recv_sem=recv_sem.at[d], device_id={"src": peer(d)}, device_id_type=MESH,
            )
        )
    order = sorted(range(1, src_count), key=lambda d: -min(d, src_count - d))
    to_right.start()
    to_left.start()
    for d in order:
        sends[d - 1].start()

    def forward(d, source):
        column = lax.rem(me + src_count - d, src_count)
        return pltpu.make_async_remote_copy(
            src_ref=source(column), dst_ref=buf.at[column, landing], send_sem=halo_send.at[d],
            recv_sem=halo_recv.at[d], device_id={"tgt": 1 - half}, device_id_type=MESH,
        )

    forwards = []
    if tgt_count > 1:
        offset = pl.multiple_of((1 - half) * (rows - HALO), HALO)
        forwards.append(forward(0, lambda column: tgt_hbm.at[pl.ds(offset, HALO)]))
        forwards[0].start()

    zero_block = jnp.zeros((span, width), BF16)
    vol[0] = zero_block
    vol[breadth + 1] = zero_block
    sec[1] = zero_block
    sec[breadth] = zero_block
    for copy in own[2:5]:
        copy.wait()
    expand = (remainder(iota((groups, width), 1), groups) == iota((groups, width), 0)).astype(BF16)
    spread = [dot(taps[i], expand).astype(BF16) for i in range(3)]
    lane_group = quotient(iota((groups, width), 1), groups)
    lane_row = remainder(lane_group, window_rows)
    nothing = jnp.zeros((groups, width), BF16)

    def tap(i, a, b):
        start = (a * 3 + b) * groups
        return spread[i][start : start + groups]

    for a in range(3):
        for b in range(3):
            for j in range(width // groups):
                w1[a, pl.ds(b * width + j * groups, groups), :] = jnp.where(
                    lane_group == j, tap(0, a, b), nothing
                )
    for j in range(width // groups):
        k, h = divmod(j, window_rows)
        two = nothing
        three = [nothing[:, :LANES]] * 3
        if k < 3:
            for a in range(3):
                two = jnp.where(lane_row == h - a + 1, tap(1, a, k), two)
                three[a] = jnp.where(
                    (lane_row == h)[:, :LANES], tap(2, a, k)[:, :LANES], three[a]
                )
        w2[pl.ds(j * groups, groups), :] = two
        for a in range(3):
            w3[pl.ds(j * groups, groups), pl.ds(a * LANES, LANES)] = three[a]

    def valid(extra):
        position = iota((span, width), 0)
        low = half * (HALO - extra)
        return ((position >= low) & (position < low + rows + extra))[None]

    valid_one, valid_two = valid(2), valid(1)

    own[1].wait()
    own[5].wait()
    own[6].wait()
    to_right.wait()
    to_left.wait()
    row_of = quotient(iota((column_lanes, map_rows), 0), groups)
    wanted = jnp.zeros((column_lanes, map_rows), jnp.int32)
    for h in range(window_rows):
        wanted = jnp.where(row_of == h, rows_ref[h], wanted)
    select = (iota((column_lanes, map_rows), 1) == wanted).astype(BF16)
    same_group = (
        quotient(iota((column_lanes, features), 1), channels)
        == remainder(iota((column_lanes, features), 0), groups)
    )
    parts = []
    for k in range(3):
        keep = same_group
        if k == 0:
            keep = keep & (me > 0)
        if k == 2:
            keep = keep & (me < src_count - 1)
        parts.append(jnp.where(keep, dot(select, sbuf[k]), 0.0).astype(BF16))
    if width > 3 * column_lanes:
        parts.append(jnp.zeros((width - 3 * column_lanes, features), BF16))
    weights = jnp.concatenate(parts, axis=0)

    own[0].wait()
    for d in range(1, src_count):
        sends[d - 1].wait_recv()
        if tgt_count > 1:
            copy = forward(d, lambda column: buf.at[column, edge])
            copy.start()
            forwards.append(copy)
    for copy in forwards:
        copy.wait_recv()

    def volume_chunk(chunk):
        window = jnp.concatenate(
            [buf[cols_ref[chunk * per_block + i]] for i in range(per_block)], axis=0
        )
        scores = lax.dot_general(
            window, weights, (((1,), (1,)), ((), ())), preferred_element_type=F32
        ) * (channels ** -0.5)
        vol[pl.ds(chunk * per_block + 1, per_block)] = jnp.where(
            valid_one, scores.reshape(per_block, span, width), 0.0
        ).astype(BF16)

    def at(ref, chunk, b):
        return ref[pl.ds(chunk * per_block + b, per_block)].reshape(chunk_rows, width)

    def shifted(parts):
        total = parts[1] + pltpu.roll(parts[0], 1, 0)
        return total + pltpu.roll(parts[2], chunk_rows - 1, 0)

    def middle_chunk(chunk):
        window = jnp.concatenate([at(vol, chunk, b) for b in range(3)], axis=1)
        one = shifted([dot(window, w1[a]) for a in range(3)])
        one = jnp.maximum(one, 0.0).astype(BF16)
        two = jnp.maximum(dot(one, w2[...]), 0.0).reshape(per_block, span, width)
        two = jnp.where(valid_two, two, 0.0).astype(BF16)
        for b in range(3):
            lanes = slice(b * column_lanes, (b + 1) * column_lanes if b < 2 else width)
            sec[pl.ds(chunk * per_block + 2 - b, per_block), :, lanes] = two[:, :, lanes]

    def last_chunk(chunk):
        three = dot(at(sec, chunk, 1), w3[...])
        three = shifted([three[:, a * LANES : (a + 1) * LANES] for a in range(3)])
        stage[...] = jnp.maximum(three, 0.0)
        pieces = [
            stage[pl.ds(pl.multiple_of(i * span + half * HALO, HALO), rows), :]
            for i in range(per_block)
        ]
        rolled = []
        for d in range(window_rows):
            mixed = pieces[d % per_block]
            for j in range(1, per_block):
                mixed = jnp.where(in_group[j], pieces[(j + d) % per_block], mixed)
            rolled.append(pltpu.roll(mixed, d * groups, 1) if d else mixed)
        for h in range(window_rows):
            total = rolled[0]
            for d in range(1, window_rows):
                total = jnp.where(in_row[(d + h) % window_rows], rolled[d], total)
            out_ref[h, :, pl.ds(pl.multiple_of(chunk * LANES, LANES), LANES)] = total.astype(BF16)

    group = quotient(iota((rows, LANES), 1), groups)
    in_group = [group == j for j in range(per_block)]
    in_row = [remainder(group, window_rows) == h for h in range(window_rows)]

    for step in (volume_chunk, middle_chunk, last_chunk):
        if chunks == 1:
            step(0)
        else:
            pl.loop(0, chunks)(step)

    for copy in sends:
        copy.wait_send()
    for copy in forwards:
        copy.wait_send()


def local(
    src_count,
    tgt_count,
    source_features,
    target_features,
    source_rows,
    target_cols,
    target_kernel_one,
    source_kernel,
    target_kernel_two,
):
    groups = source_kernel.shape[2]
    window_rows = source_rows.shape[0]
    breadth = target_cols.shape[0]
    map_rows, _, features = source_features.shape
    rows = target_features.shape[0]
    span = rows + HALO
    width = -(-3 * window_rows * groups // LANES) * LANES
    chunk_rows = LANES // groups * span
    taps = 9 * groups
    hbm = pl.BlockSpec(memory_space=pltpu.HBM)
    operands = (
        source_rows,
        target_cols,
        target_features[:, 0],
        source_features[:, 0],
        target_kernel_one.reshape(taps, groups),
        source_kernel.reshape(taps, groups),
        target_kernel_two.reshape(taps, groups),
    )
    dma = pltpu.SemaphoreType.DMA
    out = pl.pallas_call(
        functools.partial(kernel, src_count, tgt_count, breadth, window_rows, groups),
        out_shape=jax.ShapeDtypeStruct((window_rows, rows, breadth * groups), BF16),
        in_specs=[hbm] * 7,
        out_specs=pl.BlockSpec(memory_space=pltpu.VMEM),
        scratch_shapes=[
            pltpu.SMEM((window_rows,), jnp.int32),
            pltpu.SMEM((breadth,), jnp.int32),
            pltpu.VMEM((breadth, span, features), BF16),
            pltpu.VMEM((3, map_rows, features), BF16),
            pltpu.VMEM((3, taps, groups), BF16),
            pltpu.VMEM((breadth + 2, span, width), BF16),
            pltpu.VMEM((breadth + 2, span, width), BF16),
            pltpu.VMEM((chunk_rows, LANES), F32),
            pltpu.VMEM((3, 3 * width, width), BF16),
            pltpu.VMEM((width, width), BF16),
            pltpu.VMEM((width, 3 * LANES), BF16),
            dma((7,)),
            dma((src_count,)),
            dma((src_count,)),
            dma((src_count,)),
            dma((src_count,)),
            dma((2,)),
            dma((2,)),
        ],
        compiler_params=pltpu.CompilerParams(
            collective_id=0, has_side_effects=True, vmem_limit_bytes=48 * 1024 * 1024
        ),
    )(*(pltpu.with_memory_space_constraint(operand, pltpu.HBM) for operand in operands))
    return out[:, None]


def solution(mesh):
    return jax.shard_map(
        functools.partial(local, mesh.shape["src"], mesh.shape["tgt"]),
        mesh=mesh,
        in_specs=(
            P("pair", "src", None),
            P(("pair", "tgt"), "src", None),
            P("pair"),
            P("pair"),
            P(),
            P(),
            P(),
        ),
        out_specs=P("pair", "src", "tgt", None),
        check_vma=False,
    )
```

```python
import functools

import jax
import jax.numpy as jnp
from jax import lax
from jax.experimental import pallas as pl
from jax.experimental.pallas import tpu as pltpu
from jax.sharding import PartitionSpec as P

MESH = pl.DeviceIdType.MESH
LANES = 128
HALO = 16
BF16 = jnp.bfloat16
F32 = jnp.float32


def iota(shape, dim):
    return lax.broadcasted_iota(jnp.int32, shape, dim)


def quotient(x, n):
    return x >> (n.bit_length() - 1) if n & (n - 1) == 0 else x // n


def remainder(x, n):
    return x & (n - 1) if n & (n - 1) == 0 else x % n


def dot(a, b):
    return jnp.dot(a, b, preferred_element_type=F32)


def kernel(
    src_count,
    tgt_count,
    breadth,
    window_rows,
    groups,
    rows_hbm,
    cols_hbm,
    tgt_hbm,
    src_hbm,
    k1_hbm,
    ks_hbm,
    k2_hbm,
    out_ref,
    rows_ref,
    cols_ref,
    buf,
    src_map,
    sbuf,
    taps,
    rim,
    vol,
    acc,
    sec,
    stage,
    w1,
    w2,
    w3,
    local_sem,
    send_sem,
    recv_sem,
    halo_send,
    halo_recv,
    src_send,
    src_recv,
):
    rows, features = tgt_hbm.shape
    map_rows = src_hbm.shape[0]
    channels = features // groups
    span = rows + HALO
    width = vol.shape[2]
    column_lanes = window_rows * groups
    per_block = LANES // groups
    chunks = breadth // per_block
    chunk_rows = per_block * span
    me = lax.axis_index("src")
    half = lax.axis_index("tgt")
    main = pl.ds(pl.multiple_of(half * HALO, HALO), rows)

    def peer(d):
        return lax.rem(me + d, src_count)

    sbuf[0] = jnp.zeros(sbuf.shape[1:], BF16)
    sbuf[2] = jnp.zeros(sbuf.shape[1:], BF16)
    barrier = pltpu.get_barrier_semaphore()
    for d in range(1, src_count):
        pl.semaphore_signal(barrier, inc=1, device_id={"src": peer(d)}, device_id_type=MESH)
    if tgt_count > 1:
        pl.semaphore_signal(barrier, inc=1, device_id={"tgt": 1 - half}, device_id_type=MESH)

    own = [
        pltpu.make_async_copy(tgt_hbm, buf.at[me], local_sem.at[0]),
        pltpu.make_async_copy(src_hbm, src_map, local_sem.at[1]),
        pltpu.make_async_copy(k1_hbm, taps.at[0], local_sem.at[2]),
        pltpu.make_async_copy(ks_hbm, taps.at[1], local_sem.at[3]),
        pltpu.make_async_copy(k2_hbm, taps.at[2], local_sem.at[4]),
        pltpu.make_async_copy(rows_hbm, rows_ref, local_sem.at[5]),
        pltpu.make_async_copy(cols_hbm, cols_ref, local_sem.at[6]),
    ]
    for copy in own:
        copy.start()
    pl.semaphore_wait(barrier, src_count - 1 + (1 if tgt_count > 1 else 0))

    edge = pl.ds(pl.multiple_of((1 - half) * (rows - HALO), HALO), HALO)
    arrived = pl.ds(pl.multiple_of((1 - half) * rows, HALO), HALO)

    to_right = pltpu.make_async_remote_copy(
        src_ref=sbuf.at[1], dst_ref=sbuf.at[0], send_sem=src_send.at[0], recv_sem=src_recv.at[0],
        device_id={"src": lax.rem(me + 1, src_count)}, device_id_type=MESH,
    )
    to_left = pltpu.make_async_remote_copy(
        src_ref=sbuf.at[1], dst_ref=sbuf.at[2], send_sem=src_send.at[1], recv_sem=src_recv.at[1],
        device_id={"src": lax.rem(me + src_count - 1, src_count)}, device_id_type=MESH,
    )
    sends = []
    for d in range(1, src_count):
        sends.append(
            pltpu.make_async_remote_copy(
                src_ref=tgt_hbm, dst_ref=buf.at[me], send_sem=send_sem.at[d],
                recv_sem=recv_sem.at[d], device_id={"src": peer(d)}, device_id_type=MESH,
            )
        )
    order = sorted(range(1, src_count), key=lambda d: -min(d, src_count - d))
    for d in order:
        sends[d - 1].start()

    def forward(d, source):
        column = lax.rem(me + src_count - d, src_count)
        return pltpu.make_async_remote_copy(
            src_ref=source(column), dst_ref=rim.at[column], send_sem=halo_send.at[d],
            recv_sem=halo_recv.at[d], device_id={"tgt": 1 - half}, device_id_type=MESH,
        )

    forwards = []
    if tgt_count == 1:
        for column in range(breadth):
            rim[column] = jnp.zeros((HALO, features), BF16)
    else:
        offset = pl.multiple_of((1 - half) * (rows - HALO), HALO)
        forwards.append(forward(0, lambda column: tgt_hbm.at[pl.ds(offset, HALO)]))
        forwards[0].start()

    has_left, has_right = me > 0, me < src_count - 1
    own[1].wait()
    own[5].wait()
    own[6].wait()
    picked = sbuf.shape[1]
    row_of = iota((picked, map_rows), 0)
    wanted = jnp.full((picked, map_rows), -1, jnp.int32)
    for h in range(window_rows):
        wanted = jnp.where(row_of == h, rows_ref[h], wanted)
    choice = (iota((picked, map_rows), 1) == wanted).astype(BF16)
    sbuf[1] = dot(choice, src_map[...]).astype(BF16)
    pl.when(has_right)(to_right.start)
    pl.when(has_left)(to_left.start)

    zero_block = jnp.zeros((span, width), BF16)
    vol[0] = zero_block
    vol[breadth + 1] = zero_block
    sec[1] = zero_block
    sec[breadth] = zero_block
    for copy in own[2:5]:
        copy.wait()
    expand = (remainder(iota((groups, width), 1), groups) == iota((groups, width), 0)).astype(BF16)
    spread = [dot(taps[i], expand).astype(BF16) for i in range(3)]
    lane_group = quotient(iota((groups, width), 1), groups)
    lane_row = remainder(lane_group, window_rows)
    nothing = jnp.zeros((groups, width), BF16)

    def tap(i, a, b):
        start = (a * 3 + b) * groups
        return spread[i][start : start + groups]

    for a in range(3):
        for b in range(3):
            for j in range(width // groups):
                w1[a, pl.ds(b * width + j * groups, groups), :] = jnp.where(
                    lane_group == j, tap(0, a, b), nothing
                )
    for j in range(width // groups):
        k, h = divmod(j, window_rows)
        two = nothing
        three = [nothing[:, :LANES]] * 3
        if k < 3:
            for a in range(3):
                two = jnp.where(lane_row == h - a + 1, tap(1, a, k), two)
                three[a] = jnp.where(
                    (lane_row == h)[:, :LANES], tap(2, a, k)[:, :LANES], three[a]
                )
        w2[pl.ds(j * groups, groups), :] = two
        for a in range(3):
            w3[pl.ds(j * groups, groups), pl.ds(a * LANES, LANES)] = three[a]

    def valid(extra):
        position = iota((span, width), 0)
        low = half * (HALO - extra)
        return ((position >= low) & (position < low + rows + extra))[None]

    valid_two = valid(1)
    first_kept = half * (HALO - 2)
    rim_position = iota((HALO, width), 0)
    in_rim = ((rim_position >= first_kept) & (rim_position < first_kept + 2))[None]

    pl.when(has_left)(to_right.wait_recv)
    pl.when(has_right)(to_left.wait_recv)
    select = (
        quotient(iota((column_lanes, picked), 0), groups) == iota((column_lanes, picked), 1)
    ).astype(BF16)
    same_group = (
        quotient(iota((column_lanes, features), 1), channels)
        == remainder(iota((column_lanes, features), 0), groups)
    )
    parts = []
    for k in range(3):
        keep = same_group
        if k == 0:
            keep = keep & (me > 0)
        if k == 2:
            keep = keep & (me < src_count - 1)
        parts.append(jnp.where(keep, dot(select, sbuf[k]), 0.0).astype(BF16))
    if width > 3 * column_lanes:
        parts.append(jnp.zeros((width - 3 * column_lanes, features), BF16))
    weights = jnp.concatenate(parts, axis=0)

    own[0].wait()
    for d in range(1, src_count):
        sends[d - 1].wait_recv()
        if tgt_count > 1:
            copy = forward(d, lambda column: buf.at[column, edge])
            copy.start()
            forwards.append(copy)
    def volume(chunk, place, keep):
        spots = [cols_ref[chunk * per_block + i] for i in range(per_block)]
        held, spot_rows = (buf, rows) if place is main else (rim, HALO)
        window = jnp.concatenate([held[spot] for spot in spots], axis=0)
        scores = lax.dot_general(
            window, weights, (((1,), (1,)), ((), ())), preferred_element_type=F32
        ) * (channels ** -0.5)
        scores = scores.reshape(per_block, spot_rows, width)
        if keep is not None:
            scores = jnp.where(keep, scores, 0.0)
        vol[pl.ds(chunk * per_block + 1, per_block), place, :] = scores.astype(BF16)

    def sums(chunk, place):
        window = jnp.concatenate(
            [
                vol[pl.ds(chunk * per_block + b, per_block), place, :].reshape(-1, width)
                for b in range(3)
            ],
            axis=1,
        )
        for a in range(3):
            acc[a, pl.ds(chunk * per_block, per_block), place, :] = dot(window, w1[a]).reshape(
                per_block, -1, width
            )

    def main_volume(chunk):
        volume(chunk, main, None)

    def main_sums(chunk):
        sums(chunk, main)

    def rim_volume(chunk):
        volume(chunk, arrived, in_rim)

    def at(ref, chunk, b):
        return ref[pl.ds(chunk * per_block + b, per_block)].reshape(chunk_rows, width)

    def shifted(parts):
        total = parts[1] + pltpu.roll(parts[0], 1, 0)
        return total + pltpu.roll(parts[2], chunk_rows - 1, 0)

    def middle_chunk(chunk):
        sums(chunk, arrived)
        one = shifted([at(acc.at[a], chunk, 0) for a in range(3)])
        one = jnp.maximum(one, 0.0).astype(BF16)
        two = jnp.maximum(dot(one, w2[...]), 0.0).reshape(per_block, span, width)
        two = jnp.where(valid_two, two, 0.0).astype(BF16)
        for b in range(3):
            lanes = slice(b * column_lanes, (b + 1) * column_lanes if b < 2 else width)
            sec[pl.ds(chunk * per_block + 2 - b, per_block), :, lanes] = two[:, :, lanes]

    def last_chunk(chunk):
        three = dot(at(sec, chunk, 1), w3[...])
        three = shifted([three[:, a * LANES : (a + 1) * LANES] for a in range(3)])
        stage[...] = jnp.maximum(three, 0.0)
        pieces = [
            stage[pl.ds(pl.multiple_of(i * span + half * HALO, HALO), rows), :]
            for i in range(per_block)
        ]
        rolled = []
        for d in range(window_rows):
            mixed = pieces[d % per_block]
            for j in range(1, per_block):
                mixed = jnp.where(in_group[j], pieces[(j + d) % per_block], mixed)
            rolled.append(pltpu.roll(mixed, d * groups, 1) if d else mixed)
        for h in range(window_rows):
            total = rolled[0]
            for d in range(1, window_rows):
                total = jnp.where(in_row[(d + h) % window_rows], rolled[d], total)
            out_ref[h, :, pl.ds(pl.multiple_of(chunk * LANES, LANES), LANES)] = total.astype(BF16)

    group = quotient(iota((rows, LANES), 1), groups)
    in_group = [group == j for j in range(per_block)]
    in_row = [remainder(group, window_rows) == h for h in range(window_rows)]

    for step in (main_volume, main_sums, rim_volume, middle_chunk, last_chunk):
        if step is rim_volume:
            for copy in forwards:
                copy.wait_recv()
        if chunks == 1:
            step(0)
        else:
            pl.loop(0, chunks)(step)

    pl.when(has_right)(to_right.wait_send)
    pl.when(has_left)(to_left.wait_send)
    for copy in sends:
        copy.wait_send()
    for copy in forwards:
        copy.wait_send()


def local(
    src_count,
    tgt_count,
    source_features,
    target_features,
    source_rows,
    target_cols,
    target_kernel_one,
    source_kernel,
    target_kernel_two,
):
    groups = source_kernel.shape[2]
    window_rows = source_rows.shape[0]
    breadth = target_cols.shape[0]
    map_rows, _, features = source_features.shape
    rows = target_features.shape[0]
    span = rows + HALO
    width = -(-3 * window_rows * groups // LANES) * LANES
    chunk_rows = LANES // groups * span
    taps = 9 * groups
    hbm = pl.BlockSpec(memory_space=pltpu.HBM)
    operands = (
        source_rows,
        target_cols,
        target_features[:, 0],
        source_features[:, 0],
        target_kernel_one.reshape(taps, groups),
        source_kernel.reshape(taps, groups),
        target_kernel_two.reshape(taps, groups),
    )
    dma = pltpu.SemaphoreType.DMA
    out = pl.pallas_call(
        functools.partial(kernel, src_count, tgt_count, breadth, window_rows, groups),
        out_shape=jax.ShapeDtypeStruct((window_rows, rows, breadth * groups), BF16),
        in_specs=[hbm] * 7,
        out_specs=pl.BlockSpec(memory_space=pltpu.VMEM),
        scratch_shapes=[
            pltpu.SMEM((window_rows,), jnp.int32),
            pltpu.SMEM((breadth,), jnp.int32),
            pltpu.VMEM((breadth, rows, features), BF16),
            pltpu.VMEM((map_rows, features), BF16),
            pltpu.VMEM((3, -(-window_rows // 16) * 16, features), BF16),
            pltpu.VMEM((3, taps, groups), BF16),
            pltpu.VMEM((breadth, HALO, features), BF16),
            pltpu.VMEM((breadth + 2, span, width), BF16),
            pltpu.VMEM((3, breadth, span, width), F32),
            pltpu.VMEM((breadth + 2, span, width), BF16),
            pltpu.VMEM((chunk_rows, LANES), F32),
            pltpu.VMEM((3, 3 * width, width), BF16),
            pltpu.VMEM((width, width), BF16),
            pltpu.VMEM((width, 3 * LANES), BF16),
            dma((7,)),
            dma((src_count,)),
            dma((src_count,)),
            dma((src_count,)),
            dma((src_count,)),
            dma((2,)),
            dma((2,)),
        ],
        compiler_params=pltpu.CompilerParams(
            collective_id=0, has_side_effects=True, vmem_limit_bytes=48 * 1024 * 1024
        ),
    )(*(pltpu.with_memory_space_constraint(operand, pltpu.HBM) for operand in operands))
    return out[:, None]


def solution(mesh):
    return jax.shard_map(
        functools.partial(local, mesh.shape["src"], mesh.shape["tgt"]),
        mesh=mesh,
        in_specs=(
            P("pair", "src", None),
            P(("pair", "tgt"), "src", None),
            P("pair"),
            P("pair"),
            P(),
            P(),
            P(),
        ),
        out_specs=P("pair", "src", "tgt", None),
        check_vma=False,
    )
```

```python
import functools

import jax
import jax.numpy as jnp
from jax import lax
from jax.experimental import pallas as pl
from jax.experimental.pallas import tpu as pltpu
from jax.sharding import PartitionSpec as P

MESH = pl.DeviceIdType.MESH
LANES = 128
HALO = 16
BF16 = jnp.bfloat16
F32 = jnp.float32


def iota(shape, dim):
    return lax.broadcasted_iota(jnp.int32, shape, dim)


def quotient(x, n):
    return x >> (n.bit_length() - 1) if n & (n - 1) == 0 else x // n


def remainder(x, n):
    return x & (n - 1) if n & (n - 1) == 0 else x % n


def dot(a, b):
    return jnp.dot(a, b, preferred_element_type=F32)


def kernel(
    src_count,
    tgt_count,
    breadth,
    window_rows,
    groups,
    rows_hbm,
    cols_hbm,
    tgt_hbm,
    src_hbm,
    k1_hbm,
    ks_hbm,
    k2_hbm,
    out_ref,
    rows_ref,
    cols_ref,
    buf,
    src_map,
    sbuf,
    taps,
    rim,
    vol,
    acc,
    sec,
    stage,
    w1,
    w2,
    w3,
    local_sem,
    send_sem,
    recv_sem,
    relay_send,
    relay_recv,
    halo_send,
    halo_recv,
    src_send,
    src_recv,
):
    rows, features = tgt_hbm.shape
    map_rows = src_hbm.shape[0]
    channels = features // groups
    span = rows + HALO
    width = vol.shape[2]
    column_lanes = window_rows * groups
    per_block = LANES // groups
    chunks = breadth // per_block
    chunk_rows = per_block * span
    me = lax.axis_index("src")
    half = lax.axis_index("tgt")
    main = pl.ds(pl.multiple_of(half * HALO, HALO), rows)

    lines = src_count // 2
    side = lax.rem(me, 2)
    rank = me // 2
    mate = me + 1 - 2 * side
    beyond = lax.rem(me + src_count - 1 + 2 * side, src_count)

    def peer(d):
        if lines & (lines - 1):
            return lax.rem(rank + d, lines) * 2 + side
        other = rank
        for bit in range(d.bit_length()):
            if d >> bit & 1:
                other = other + (1 << bit) * (1 - 2 * lax.rem(rank // (1 << bit), 2))
        return other * 2 + side

    def sender(d):
        if lines & (lines - 1):
            return lax.rem(rank + lines - d, lines) * 2 + side
        return peer(d)

    sbuf[0] = jnp.zeros(sbuf.shape[1:], BF16)
    sbuf[2] = jnp.zeros(sbuf.shape[1:], BF16)
    barrier = pltpu.get_barrier_semaphore()
    greeted = [peer(d) for d in range(1, lines)] + [mate, beyond]
    for other in greeted:
        pl.semaphore_signal(barrier, inc=1, device_id={"src": other}, device_id_type=MESH)
    if tgt_count > 1:
        pl.semaphore_signal(barrier, inc=1, device_id={"tgt": 1 - half}, device_id_type=MESH)

    own = [
        pltpu.make_async_copy(tgt_hbm, buf.at[me], local_sem.at[0]),
        pltpu.make_async_copy(src_hbm, src_map, local_sem.at[1]),
        pltpu.make_async_copy(k1_hbm, taps.at[0], local_sem.at[2]),
        pltpu.make_async_copy(ks_hbm, taps.at[1], local_sem.at[3]),
        pltpu.make_async_copy(k2_hbm, taps.at[2], local_sem.at[4]),
        pltpu.make_async_copy(rows_hbm, rows_ref, local_sem.at[5]),
        pltpu.make_async_copy(cols_hbm, cols_ref, local_sem.at[6]),
    ]
    for copy in own:
        copy.start()
    pl.semaphore_wait(barrier, len(greeted) + (1 if tgt_count > 1 else 0))

    edge = pl.ds(pl.multiple_of((1 - half) * (rows - HALO), HALO), HALO)
    arrived = pl.ds(pl.multiple_of((1 - half) * rows, HALO), HALO)

    to_right = pltpu.make_async_remote_copy(
        src_ref=sbuf.at[1], dst_ref=sbuf.at[0], send_sem=src_send.at[0], recv_sem=src_recv.at[0],
        device_id={"src": lax.rem(me + 1, src_count)}, device_id_type=MESH,
    )
    to_left = pltpu.make_async_remote_copy(
        src_ref=sbuf.at[1], dst_ref=sbuf.at[2], send_sem=src_send.at[1], recv_sem=src_recv.at[1],
        device_id={"src": lax.rem(me + src_count - 1, src_count)}, device_id_type=MESH,
    )
    sends = []
    for d in list(range(1, lines)) + [0]:
        sends.append(
            pltpu.make_async_remote_copy(
                src_ref=tgt_hbm, dst_ref=buf.at[me], send_sem=send_sem.at[d],
                recv_sem=recv_sem.at[d], device_id={"src": peer(d) if d else mate},
                device_id_type=MESH,
            )
        )
    for copy in sends:
        copy.start()

    def forward(slot, column, source):
        return pltpu.make_async_remote_copy(
            src_ref=source, dst_ref=rim.at[column], send_sem=halo_send.at[slot],
            recv_sem=halo_recv.at[slot], device_id={"tgt": 1 - half}, device_id_type=MESH,
        )

    forwards = []

    def pass_edge(slot, column, source):
        if tgt_count > 1:
            copy = forward(slot, column, source)
            copy.start()
            forwards.append(copy)

    if tgt_count == 1:
        for column in range(breadth):
            rim[column] = jnp.zeros((HALO, features), BF16)
    offset = pl.multiple_of((1 - half) * (rows - HALO), HALO)
    pass_edge(0, me, tgt_hbm.at[pl.ds(offset, HALO)])

    has_left, has_right = me > 0, me < src_count - 1
    own[1].wait()
    own[5].wait()
    own[6].wait()
    picked = sbuf.shape[1]
    row_of = iota((picked, map_rows), 0)
    wanted = jnp.full((picked, map_rows), -1, jnp.int32)
    for h in range(window_rows):
        wanted = jnp.where(row_of == h, rows_ref[h], wanted)
    choice = (iota((picked, map_rows), 1) == wanted).astype(BF16)
    sbuf[1] = dot(choice, src_map[...]).astype(BF16)
    pl.when(has_right)(to_right.start)
    pl.when(has_left)(to_left.start)

    zero_block = jnp.zeros((span, width), BF16)
    vol[0] = zero_block
    vol[breadth + 1] = zero_block
    sec[1] = zero_block
    sec[breadth] = zero_block
    for copy in own[2:5]:
        copy.wait()
    expand = (remainder(iota((groups, width), 1), groups) == iota((groups, width), 0)).astype(BF16)
    spread = [dot(taps[i], expand).astype(BF16) for i in range(3)]
    lane_group = quotient(iota((groups, width), 1), groups)
    lane_row = remainder(lane_group, window_rows)
    nothing = jnp.zeros((groups, width), BF16)

    def tap(i, a, b):
        start = (a * 3 + b) * groups
        return spread[i][start : start + groups]

    for a in range(3):
        for b in range(3):
            for j in range(width // groups):
                w1[a, pl.ds(b * width + j * groups, groups), :] = jnp.where(
                    lane_group == j, tap(0, a, b), nothing
                )
    for j in range(width // groups):
        k, h = divmod(j, window_rows)
        two = nothing
        three = [nothing[:, :LANES]] * 3
        if k < 3:
            for a in range(3):
                two = jnp.where(lane_row == h - a + 1, tap(1, a, k), two)
                three[a] = jnp.where(
                    (lane_row == h)[:, :LANES], tap(2, a, k)[:, :LANES], three[a]
                )
        w2[pl.ds(j * groups, groups), :] = two
        for a in range(3):
            w3[pl.ds(j * groups, groups), pl.ds(a * LANES, LANES)] = three[a]

    def valid(extra):
        position = iota((span, width), 0)
        low = half * (HALO - extra)
        return ((position >= low) & (position < low + rows + extra))[None]

    valid_two = valid(1)
    first_kept = half * (HALO - 2)
    rim_position = iota((HALO, width), 0)
    in_rim = ((rim_position >= first_kept) & (rim_position < first_kept + 2))[None]

    relays = []
    for d in range(1, lines):
        sends[d - 1].wait_recv()
        column = sender(d)
        relay = pltpu.make_async_remote_copy(
            src_ref=buf.at[column], dst_ref=buf.at[column], send_sem=relay_send.at[d],
            recv_sem=relay_recv.at[d], device_id={"src": mate}, device_id_type=MESH,
        )
        relay.start()
        relays.append(relay)
        pass_edge(d, column, buf.at[column, edge])
    sends[-1].wait_recv()
    pass_edge(lines, mate, buf.at[mate, edge])

    pl.when(has_left)(to_right.wait_recv)
    pl.when(has_right)(to_left.wait_recv)
    select = (
        quotient(iota((column_lanes, picked), 0), groups) == iota((column_lanes, picked), 1)
    ).astype(BF16)
    same_group = (
        quotient(iota((column_lanes, features), 1), channels)
        == remainder(iota((column_lanes, features), 0), groups)
    )
    parts = []
    for k in range(3):
        keep = same_group
        if k == 0:
            keep = keep & (me > 0)
        if k == 2:
            keep = keep & (me < src_count - 1)
        parts.append(jnp.where(keep, dot(select, sbuf[k]), 0.0).astype(BF16))
    if width > 3 * column_lanes:
        parts.append(jnp.zeros((width - 3 * column_lanes, features), BF16))
    weights = jnp.concatenate(parts, axis=0)

    own[0].wait()
    for d in range(1, lines):
        relays[d - 1].wait_recv()
        column = sender(d) + 1 - 2 * side
        pass_edge(lines + d, column, buf.at[column, edge])

    def volume(chunk, place, keep):
        spots = [cols_ref[chunk * per_block + i] for i in range(per_block)]
        held, spot_rows = (buf, rows) if place is main else (rim, HALO)
        window = jnp.concatenate([held[spot] for spot in spots], axis=0)
        scores = lax.dot_general(
            window, weights, (((1,), (1,)), ((), ())), preferred_element_type=F32
        ) * (channels ** -0.5)
        scores = scores.reshape(per_block, spot_rows, width)
        if keep is not None:
            scores = jnp.where(keep, scores, 0.0)
        vol[pl.ds(chunk * per_block + 1, per_block), place, :] = scores.astype(BF16)

    def sums(chunk, place):
        window = jnp.concatenate(
            [
                vol[pl.ds(chunk * per_block + b, per_block), place, :].reshape(-1, width)
                for b in range(3)
            ],
            axis=1,
        )
        for a in range(3):
            acc[a, pl.ds(chunk * per_block, per_block), place, :] = dot(window, w1[a]).reshape(
                per_block, -1, width
            )

    def main_volume(chunk):
        volume(chunk, main, None)

    def main_sums(chunk):
        sums(chunk, main)

    def rim_volume(chunk):
        volume(chunk, arrived, in_rim)

    def at(ref, chunk, b):
        return ref[pl.ds(chunk * per_block + b, per_block)].reshape(chunk_rows, width)

    def shifted(parts):
        total = parts[1] + pltpu.roll(parts[0], 1, 0)
        return total + pltpu.roll(parts[2], chunk_rows - 1, 0)

    def middle_chunk(chunk):
        sums(chunk, arrived)
        one = shifted([at(acc.at[a], chunk, 0) for a in range(3)])
        one = jnp.maximum(one, 0.0).astype(BF16)
        two = jnp.maximum(dot(one, w2[...]), 0.0).reshape(per_block, span, width)
        two = jnp.where(valid_two, two, 0.0).astype(BF16)
        for b in range(3):
            lanes = slice(b * column_lanes, (b + 1) * column_lanes if b < 2 else width)
            sec[pl.ds(chunk * per_block + 2 - b, per_block), :, lanes] = two[:, :, lanes]

    def last_chunk(chunk):
        three = dot(at(sec, chunk, 1), w3[...])
        three = shifted([three[:, a * LANES : (a + 1) * LANES] for a in range(3)])
        stage[...] = jnp.maximum(three, 0.0)
        pieces = [
            stage[pl.ds(pl.multiple_of(i * span + half * HALO, HALO), rows), :]
            for i in range(per_block)
        ]
        rolled = []
        for d in range(window_rows):
            mixed = pieces[d % per_block]
            for j in range(1, per_block):
                mixed = jnp.where(in_group[j], pieces[(j + d) % per_block], mixed)
            rolled.append(pltpu.roll(mixed, d * groups, 1) if d else mixed)
        for h in range(window_rows):
            total = rolled[0]
            for d in range(1, window_rows):
                total = jnp.where(in_row[(d + h) % window_rows], rolled[d], total)
            out_ref[h, :, pl.ds(pl.multiple_of(chunk * LANES, LANES), LANES)] = total.astype(BF16)

    group = quotient(iota((rows, LANES), 1), groups)
    in_group = [group == j for j in range(per_block)]
    in_row = [remainder(group, window_rows) == h for h in range(window_rows)]

    for step in (main_volume, main_sums, rim_volume, middle_chunk, last_chunk):
        if step is rim_volume:
            for copy in forwards:
                copy.wait_recv()
        if chunks == 1:
            step(0)
        else:
            pl.loop(0, chunks)(step)

    pl.when(has_right)(to_right.wait_send)
    pl.when(has_left)(to_left.wait_send)
    for copy in sends + relays:
        copy.wait_send()
    for copy in forwards:
        copy.wait_send()


def local(
    src_count,
    tgt_count,
    source_features,
    target_features,
    source_rows,
    target_cols,
    target_kernel_one,
    source_kernel,
    target_kernel_two,
):
    groups = source_kernel.shape[2]
    window_rows = source_rows.shape[0]
    breadth = target_cols.shape[0]
    map_rows, _, features = source_features.shape
    rows = target_features.shape[0]
    span = rows + HALO
    width = -(-3 * window_rows * groups // LANES) * LANES
    chunk_rows = LANES // groups * span
    taps = 9 * groups
    hbm = pl.BlockSpec(memory_space=pltpu.HBM)
    operands = (
        source_rows,
        target_cols,
        target_features[:, 0],
        source_features[:, 0],
        target_kernel_one.reshape(taps, groups),
        source_kernel.reshape(taps, groups),
        target_kernel_two.reshape(taps, groups),
    )
    dma = pltpu.SemaphoreType.DMA
    out = pl.pallas_call(
        functools.partial(kernel, src_count, tgt_count, breadth, window_rows, groups),
        out_shape=jax.ShapeDtypeStruct((window_rows, rows, breadth * groups), BF16),
        in_specs=[hbm] * 7,
        out_specs=pl.BlockSpec(memory_space=pltpu.VMEM),
        scratch_shapes=[
            pltpu.SMEM((window_rows,), jnp.int32),
            pltpu.SMEM((breadth,), jnp.int32),
            pltpu.VMEM((breadth, rows, features), BF16),
            pltpu.VMEM((map_rows, features), BF16),
            pltpu.VMEM((3, -(-window_rows // 16) * 16, features), BF16),
            pltpu.VMEM((3, taps, groups), BF16),
            pltpu.VMEM((breadth, HALO, features), BF16),
            pltpu.VMEM((breadth + 2, span, width), BF16),
            pltpu.VMEM((3, breadth, span, width), F32),
            pltpu.VMEM((breadth + 2, span, width), BF16),
            pltpu.VMEM((chunk_rows, LANES), F32),
            pltpu.VMEM((3, 3 * width, width), BF16),
            pltpu.VMEM((width, width), BF16),
            pltpu.VMEM((width, 3 * LANES), BF16),
            dma((7,)),
            dma((src_count // 2,)),
            dma((src_count // 2,)),
            dma((src_count // 2,)),
            dma((src_count // 2,)),
            dma((src_count,)),
            dma((src_count,)),
            dma((2,)),
            dma((2,)),
        ],
        compiler_params=pltpu.CompilerParams(
            collective_id=0, has_side_effects=True, vmem_limit_bytes=48 * 1024 * 1024
        ),
    )(*(pltpu.with_memory_space_constraint(operand, pltpu.HBM) for operand in operands))
    return out[:, None]


def solution(mesh):
    return jax.shard_map(
        functools.partial(local, mesh.shape["src"], mesh.shape["tgt"]),
        mesh=mesh,
        in_specs=(
            P("pair", "src", None),
            P(("pair", "tgt"), "src", None),
            P("pair"),
            P("pair"),
            P(),
            P(),
            P(),
        ),
        out_specs=P("pair", "src", "tgt", None),
        check_vma=False,
    )
```

```python
import functools

import jax
import jax.numpy as jnp
from jax import lax
from jax.experimental import pallas as pl
from jax.experimental.pallas import tpu as pltpu
from jax.sharding import PartitionSpec as P

MESH = pl.DeviceIdType.MESH
LANES = 128
HALO = 16
BF16 = jnp.bfloat16
F32 = jnp.float32


def iota(shape, dim):
    return lax.broadcasted_iota(jnp.int32, shape, dim)


def quotient(x, n):
    return x >> (n.bit_length() - 1) if n & (n - 1) == 0 else x // n


def remainder(x, n):
    return x & (n - 1) if n & (n - 1) == 0 else x % n


def dot(a, b):
    return jnp.dot(a, b, preferred_element_type=F32)


def kernel(
    src_count,
    tgt_count,
    breadth,
    window_rows,
    groups,
    rows_hbm,
    cols_hbm,
    tgt_hbm,
    src_hbm,
    k1_hbm,
    ks_hbm,
    k2_hbm,
    out_ref,
    rows_ref,
    cols_ref,
    buf,
    sbuf,
    taps,
    vol,
    sec,
    stage,
    w1,
    w2,
    w3,
    local_sem,
    send_sem,
    recv_sem,
    halo_send,
    halo_recv,
    src_send,
    src_recv,
):
    rows, features = tgt_hbm.shape
    map_rows = src_hbm.shape[0]
    channels = features // groups
    span = rows + HALO
    width = vol.shape[2]
    column_lanes = window_rows * groups
    per_block = LANES // groups
    chunks = breadth // per_block
    chunk_rows = per_block * span
    me = lax.axis_index("src")
    half = lax.axis_index("tgt")
    main = pl.ds(pl.multiple_of(half * HALO, HALO), rows)

    def peer(d):
        return lax.rem(me + d, src_count)

    sbuf[0] = jnp.zeros(sbuf.shape[1:], BF16)
    sbuf[2] = jnp.zeros(sbuf.shape[1:], BF16)
    barrier = pltpu.get_barrier_semaphore()
    for d in range(1, src_count):
        pl.semaphore_signal(barrier, inc=1, device_id={"src": peer(d)}, device_id_type=MESH)
    if tgt_count > 1:
        for d in range(src_count):
            pl.semaphore_signal(
                barrier, inc=1, device_id={"src": peer(d), "tgt": 1 - half}, device_id_type=MESH
            )

    own = [
        pltpu.make_async_copy(tgt_hbm, buf.at[me, main], local_sem.at[0]),
        pltpu.make_async_copy(src_hbm, sbuf.at[1], local_sem.at[1]),
        pltpu.make_async_copy(k1_hbm, taps.at[0], local_sem.at[2]),
        pltpu.make_async_copy(ks_hbm, taps.at[1], local_sem.at[3]),
        pltpu.make_async_copy(k2_hbm, taps.at[2], local_sem.at[4]),
        pltpu.make_async_copy(rows_hbm, rows_ref, local_sem.at[5]),
        pltpu.make_async_copy(cols_hbm, cols_ref, local_sem.at[6]),
    ]
    for copy in own:
        copy.start()
    pl.semaphore_wait(barrier, src_count - 1 + (src_count if tgt_count > 1 else 0))

    landing = pl.ds(pl.multiple_of(half * rows, HALO), HALO)

    to_right = pltpu.make_async_remote_copy(
        src_ref=src_hbm, dst_ref=sbuf.at[0], send_sem=src_send.at[0], recv_sem=src_recv.at[0],
        device_id={"src": lax.rem(me + 1, src_count)}, device_id_type=MESH,
    )
    to_left = pltpu.make_async_remote_copy(
        src_ref=src_hbm, dst_ref=sbuf.at[2], send_sem=src_send.at[1], recv_sem=src_recv.at[1],
        device_id={"src": lax.rem(me + src_count - 1, src_count)}, device_id_type=MESH,
    )
    sends = []
    for d in range(1, src_count):
        sends.append(
            pltpu.make_async_remote_copy(
                src_ref=tgt_hbm, dst_ref=buf.at[me, main], send_sem=send_sem.at[d],
                recv_sem=recv_sem.at[d], device_id={"src": peer(d)}, device_id_type=MESH,
            )
        )
    order = sorted(range(1, src_count), key=lambda d: -min(d, src_count - d))
    has_left, has_right = me > 0, me < src_count - 1
    pl.when(has_right)(to_right.start)
    pl.when(has_left)(to_left.start)
    offset = pl.multiple_of((1 - half) * (rows - HALO), HALO)
    rims = []
    if tgt_count > 1:
        for d in range(src_count):
            rims.append(
                pltpu.make_async_remote_copy(
                    src_ref=tgt_hbm.at[pl.ds(offset, HALO)], dst_ref=buf.at[me, landing],
                    send_sem=halo_send.at[d], recv_sem=halo_recv.at[d],
                    device_id={"src": peer(d), "tgt": 1 - half}, device_id_type=MESH,
                )
            )
    for d in order:
        sends[d - 1].start()
        if rims:
            rims[d].start()
    if rims:
        rims[0].start()

    zero_block = jnp.zeros((span, width), BF16)
    vol[0] = zero_block
    vol[breadth + 1] = zero_block
    sec[1] = zero_block
    sec[breadth] = zero_block
    for copy in own[2:5]:
        copy.wait()
    expand = (remainder(iota((groups, width), 1), groups) == iota((groups, width), 0)).astype(BF16)
    spread = [dot(taps[i], expand).astype(BF16) for i in range(3)]
    lane_group = quotient(iota((groups, width), 1), groups)
    lane_row = remainder(lane_group, window_rows)
    nothing = jnp.zeros((groups, width), BF16)

    def tap(i, a, b):
        start = (a * 3 + b) * groups
        return spread[i][start : start + groups]

    for a in range(3):
        for b in range(3):
            for j in range(width // groups):
                w1[a, pl.ds(b * width + j * groups, groups), :] = jnp.where(
                    lane_group == j, tap(0, a, b), nothing
                )
    for j in range(width // groups):
        k, h = divmod(j, window_rows)
        two = nothing
        three = [nothing[:, :LANES]] * 3
        if k < 3:
            for a in range(3):
                two = jnp.where(lane_row == h - a + 1, tap(1, a, k), two)
                three[a] = jnp.where(
                    (lane_row == h)[:, :LANES], tap(2, a, k)[:, :LANES], three[a]
                )
        w2[pl.ds(j * groups, groups), :] = two
        for a in range(3):
            w3[pl.ds(j * groups, groups), pl.ds(a * LANES, LANES)] = three[a]

    def valid(extra):
        position = iota((span, width), 0)
        low = half * (HALO - extra)
        return ((position >= low) & (position < low + rows + extra))[None]

    valid_one, valid_two = valid(2), valid(1)

    own[1].wait()
    own[5].wait()
    own[6].wait()
    pl.when(has_left)(to_right.wait_recv)
    pl.when(has_right)(to_left.wait_recv)
    row_of = quotient(iota((column_lanes, map_rows), 0), groups)
    wanted = jnp.zeros((column_lanes, map_rows), jnp.int32)
    for h in range(window_rows):
        wanted = jnp.where(row_of == h, rows_ref[h], wanted)
    select = (iota((column_lanes, map_rows), 1) == wanted).astype(BF16)
    same_group = (
        quotient(iota((column_lanes, features), 1), channels)
        == remainder(iota((column_lanes, features), 0), groups)
    )
    parts = []
    for k in range(3):
        keep = same_group
        if k == 0:
            keep = keep & (me > 0)
        if k == 2:
            keep = keep & (me < src_count - 1)
        parts.append(jnp.where(keep, dot(select, sbuf[k]), 0.0).astype(BF16))
    if width > 3 * column_lanes:
        parts.append(jnp.zeros((width - 3 * column_lanes, features), BF16))
    weights = jnp.concatenate(parts, axis=0)

    own[0].wait()
    for copy in sends + rims:
        copy.wait_recv()

    def volume_chunk(chunk):
        window = jnp.concatenate(
            [buf[cols_ref[chunk * per_block + i]] for i in range(per_block)], axis=0
        )
        scores = lax.dot_general(
            window, weights, (((1,), (1,)), ((), ())), preferred_element_type=F32
        ) * (channels ** -0.5)
        vol[pl.ds(chunk * per_block + 1, per_block)] = jnp.where(
            valid_one, scores.reshape(per_block, span, width), 0.0
        ).astype(BF16)

    def at(ref, chunk, b):
        return ref[pl.ds(chunk * per_block + b, per_block)].reshape(chunk_rows, width)

    def shifted(parts):
        total = parts[1] + pltpu.roll(parts[0], 1, 0)
        return total + pltpu.roll(parts[2], chunk_rows - 1, 0)

    def middle_chunk(chunk):
        window = jnp.concatenate([at(vol, chunk, b) for b in range(3)], axis=1)
        one = shifted([dot(window, w1[a]) for a in range(3)])
        one = jnp.maximum(one, 0.0).astype(BF16)
        two = jnp.maximum(dot(one, w2[...]), 0.0).reshape(per_block, span, width)
        two = jnp.where(valid_two, two, 0.0).astype(BF16)
        for b in range(3):
            lanes = slice(b * column_lanes, (b + 1) * column_lanes if b < 2 else width)
            sec[pl.ds(chunk * per_block + 2 - b, per_block), :, lanes] = two[:, :, lanes]

    def last_chunk(chunk):
        three = dot(at(sec, chunk, 1), w3[...])
        three = shifted([three[:, a * LANES : (a + 1) * LANES] for a in range(3)])
        stage[...] = jnp.maximum(three, 0.0)
        pieces = [
            stage[pl.ds(pl.multiple_of(i * span + half * HALO, HALO), rows), :]
            for i in range(per_block)
        ]
        rolled = []
        for d in range(window_rows):
            mixed = pieces[d % per_block]
            for j in range(1, per_block):
                mixed = jnp.where(in_group[j], pieces[(j + d) % per_block], mixed)
            rolled.append(pltpu.roll(mixed, d * groups, 1) if d else mixed)
        for h in range(window_rows):
            total = rolled[0]
            for d in range(1, window_rows):
                total = jnp.where(in_row[(d + h) % window_rows], rolled[d], total)
            out_ref[h, :, pl.ds(pl.multiple_of(chunk * LANES, LANES), LANES)] = total.astype(BF16)

    group = quotient(iota((rows, LANES), 1), groups)
    in_group = [group == j for j in range(per_block)]
    in_row = [remainder(group, window_rows) == h for h in range(window_rows)]

    for step in (volume_chunk, middle_chunk, last_chunk):
        if chunks == 1:
            step(0)
        else:
            pl.loop(0, chunks)(step)

    pl.when(has_right)(to_right.wait_send)
    pl.when(has_left)(to_left.wait_send)
    for copy in sends + rims:
        copy.wait_send()


def local(
    src_count,
    tgt_count,
    source_features,
    target_features,
    source_rows,
    target_cols,
    target_kernel_one,
    source_kernel,
    target_kernel_two,
):
    groups = source_kernel.shape[2]
    window_rows = source_rows.shape[0]
    breadth = target_cols.shape[0]
    map_rows, _, features = source_features.shape
    rows = target_features.shape[0]
    span = rows + HALO
    width = -(-3 * window_rows * groups // LANES) * LANES
    chunk_rows = LANES // groups * span
    taps = 9 * groups
    hbm = pl.BlockSpec(memory_space=pltpu.HBM)
    operands = (
        source_rows,
        target_cols,
        target_features[:, 0],
        source_features[:, 0],
        target_kernel_one.reshape(taps, groups),
        source_kernel.reshape(taps, groups),
        target_kernel_two.reshape(taps, groups),
    )
    dma = pltpu.SemaphoreType.DMA
    out = pl.pallas_call(
        functools.partial(kernel, src_count, tgt_count, breadth, window_rows, groups),
        out_shape=jax.ShapeDtypeStruct((window_rows, rows, breadth * groups), BF16),
        in_specs=[hbm] * 7,
        out_specs=pl.BlockSpec(memory_space=pltpu.VMEM),
        scratch_shapes=[
            pltpu.SMEM((window_rows,), jnp.int32),
            pltpu.SMEM((breadth,), jnp.int32),
            pltpu.VMEM((breadth, span, features), BF16),
            pltpu.VMEM((3, map_rows, features), BF16),
            pltpu.VMEM((3, taps, groups), BF16),
            pltpu.VMEM((breadth + 2, span, width), BF16),
            pltpu.VMEM((breadth + 2, span, width), BF16),
            pltpu.VMEM((chunk_rows, LANES), F32),
            pltpu.VMEM((3, 3 * width, width), BF16),
            pltpu.VMEM((width, width), BF16),
            pltpu.VMEM((width, 3 * LANES), BF16),
            dma((7,)),
            dma((src_count,)),
            dma((src_count,)),
            dma((src_count,)),
            dma((src_count,)),
            dma((2,)),
            dma((2,)),
        ],
        compiler_params=pltpu.CompilerParams(
            collective_id=0, has_side_effects=True, vmem_limit_bytes=48 * 1024 * 1024
        ),
    )(*(pltpu.with_memory_space_constraint(operand, pltpu.HBM) for operand in operands))
    return out[:, None]


def solution(mesh):
    return jax.shard_map(
        functools.partial(local, mesh.shape["src"], mesh.shape["tgt"]),
        mesh=mesh,
        in_specs=(
            P("pair", "src", None),
            P(("pair", "tgt"), "src", None),
            P("pair"),
            P("pair"),
            P(),
            P(),
            P(),
        ),
        out_specs=P("pair", "src", "tgt", None),
        check_vma=False,
    )
```

```python
import functools

import jax
import jax.numpy as jnp
from jax import lax
from jax.experimental import pallas as pl
from jax.experimental.pallas import tpu as pltpu
from jax.sharding import PartitionSpec as P

MESH = pl.DeviceIdType.MESH
LANES = 128
HALO = 16
BF16 = jnp.bfloat16
F32 = jnp.float32


def iota(shape, dim):
    return lax.broadcasted_iota(jnp.int32, shape, dim)


def quotient(x, n):
    return x >> (n.bit_length() - 1) if n & (n - 1) == 0 else x // n


def remainder(x, n):
    return x & (n - 1) if n & (n - 1) == 0 else x % n


def dot(a, b):
    return jnp.dot(a, b, preferred_element_type=F32)


def kernel(
    src_count,
    tgt_count,
    breadth,
    window_rows,
    groups,
    rows_hbm,
    cols_hbm,
    tgt_hbm,
    src_hbm,
    k1_hbm,
    ks_hbm,
    k2_hbm,
    out_ref,
    rows_ref,
    cols_ref,
    buf,
    src_map,
    sbuf,
    taps,
    rim,
    vol,
    acc,
    sec,
    stage,
    w1,
    w2,
    w3,
    diagonal,
    row_masks,
    local_sem,
    send_sem,
    recv_sem,
    halo_send,
    halo_recv,
    src_send,
    src_recv,
):
    rows, features = tgt_hbm.shape
    map_rows = src_hbm.shape[0]
    channels = features // groups
    span = rows + HALO
    width = vol.shape[2]
    column_lanes = window_rows * groups
    per_block = LANES // groups
    chunks = breadth // per_block
    chunk_rows = per_block * span
    me = lax.axis_index("src")
    half = lax.axis_index("tgt")
    main = pl.ds(pl.multiple_of(half * HALO, HALO), rows)

    def peer(d):
        return lax.rem(me + d, src_count)

    sbuf[0] = jnp.zeros(sbuf.shape[1:], BF16)
    sbuf[2] = jnp.zeros(sbuf.shape[1:], BF16)
    barrier = pltpu.get_barrier_semaphore()
    for d in range(1, src_count):
        pl.semaphore_signal(barrier, inc=1, device_id={"src": peer(d)}, device_id_type=MESH)
    if tgt_count > 1:
        pl.semaphore_signal(barrier, inc=1, device_id={"tgt": 1 - half}, device_id_type=MESH)

    own = [
        pltpu.make_async_copy(tgt_hbm, buf.at[me], local_sem.at[0]),
        pltpu.make_async_copy(src_hbm, src_map, local_sem.at[1]),
        pltpu.make_async_copy(k1_hbm, taps.at[0], local_sem.at[2]),
        pltpu.make_async_copy(ks_hbm, taps.at[1], local_sem.at[3]),
        pltpu.make_async_copy(k2_hbm, taps.at[2], local_sem.at[4]),
        pltpu.make_async_copy(rows_hbm, rows_ref, local_sem.at[5]),
        pltpu.make_async_copy(cols_hbm, cols_ref, local_sem.at[6]),
    ]
    for copy in own:
        copy.start()
    zero_block = jnp.zeros((span, width), BF16)
    vol[0] = zero_block
    vol[breadth + 1] = zero_block
    sec[1] = zero_block
    sec[breadth] = zero_block
    expand = (remainder(iota((groups, width), 1), groups) == iota((groups, width), 0)).astype(BF16)
    lane_group = quotient(iota((groups, width), 1), groups)
    lane_row = remainder(lane_group, window_rows)
    nothing = jnp.zeros((groups, width), BF16)

    one = jnp.ones((groups, width), BF16)
    for j in range(width // groups):
        diagonal[pl.ds(j * groups, groups), :] = jnp.where(lane_group == j, one, nothing)
    for h in range(-1, window_rows + 1):
        row_masks[h + 1] = jnp.where(lane_row == h, one, nothing)
    pl.semaphore_wait(barrier, src_count - 1 + (1 if tgt_count > 1 else 0))

    edge = pl.ds(pl.multiple_of((1 - half) * (rows - HALO), HALO), HALO)
    arrived = pl.ds(pl.multiple_of((1 - half) * rows, HALO), HALO)

    to_right = pltpu.make_async_remote_copy(
        src_ref=sbuf.at[1], dst_ref=sbuf.at[0], send_sem=src_send.at[0], recv_sem=src_recv.at[0],
        device_id={"src": lax.rem(me + 1, src_count)}, device_id_type=MESH,
    )
    to_left = pltpu.make_async_remote_copy(
        src_ref=sbuf.at[1], dst_ref=sbuf.at[2], send_sem=src_send.at[1], recv_sem=src_recv.at[1],
        device_id={"src": lax.rem(me + src_count - 1, src_count)}, device_id_type=MESH,
    )
    sends = []
    for d in range(1, src_count):
        sends.append(
            pltpu.make_async_remote_copy(
                src_ref=tgt_hbm, dst_ref=buf.at[me], send_sem=send_sem.at[d],
                recv_sem=recv_sem.at[d], device_id={"src": peer(d)}, device_id_type=MESH,
            )
        )
    order = sorted(range(1, src_count), key=lambda d: -min(d, src_count - d))
    for d in order:
        sends[d - 1].start()

    def forward(d, source):
        column = lax.rem(me + src_count - d, src_count)
        return pltpu.make_async_remote_copy(
            src_ref=source(column), dst_ref=rim.at[column], send_sem=halo_send.at[d],
            recv_sem=halo_recv.at[d], device_id={"tgt": 1 - half}, device_id_type=MESH,
        )

    forwards = []
    if tgt_count == 1:
        for column in range(breadth):
            rim[column] = jnp.zeros((HALO, features), BF16)
    else:
        offset = pl.multiple_of((1 - half) * (rows - HALO), HALO)
        forwards.append(forward(0, lambda column: tgt_hbm.at[pl.ds(offset, HALO)]))
        forwards[0].start()

    has_left, has_right = me > 0, me < src_count - 1
    own[1].wait()
    own[5].wait()
    own[6].wait()
    picked = sbuf.shape[1]
    row_of = iota((picked, map_rows), 0)
    wanted = jnp.full((picked, map_rows), -1, jnp.int32)
    for h in range(window_rows):
        wanted = jnp.where(row_of == h, rows_ref[h], wanted)
    choice = (iota((picked, map_rows), 1) == wanted).astype(BF16)
    sbuf[1] = dot(choice, src_map[...]).astype(BF16)
    pl.when(has_right)(to_right.start)
    pl.when(has_left)(to_left.start)

    for copy in own[2:5]:
        copy.wait()
    spread = [dot(taps[i], expand).astype(BF16) for i in range(3)]
    def tap(i, a, b):
        start = (a * 3 + b) * groups
        return spread[i][start : start + groups]

    for a in range(3):
        for b in range(3):
            for j in range(width // groups):
                w1[a, pl.ds(b * width + j * groups, groups), :] = (
                    tap(0, a, b) * diagonal[pl.ds(j * groups, groups), :]
                )
    for j in range(width // groups):
        k, h = divmod(j, window_rows)
        two = nothing
        three = [nothing[:, :LANES]] * 3
        if k < 3:
            for a in range(3):
                two = two + tap(1, a, k) * row_masks[h - a + 2]
                three[a] = tap(2, a, k)[:, :LANES] * row_masks[h + 1][:, :LANES]
        w2[pl.ds(j * groups, groups), :] = two
        for a in range(3):
            w3[pl.ds(j * groups, groups), pl.ds(a * LANES, LANES)] = three[a]

    def valid(extra):
        position = iota((span, width), 0)
        low = half * (HALO - extra)
        return ((position >= low) & (position < low + rows + extra))[None]

    valid_two = valid(1)
    first_kept = half * (HALO - 2)
    rim_position = iota((HALO, width), 0)
    in_rim = ((rim_position >= first_kept) & (rim_position < first_kept + 2))[None]

    pl.when(has_left)(to_right.wait_recv)
    pl.when(has_right)(to_left.wait_recv)
    select = (
        quotient(iota((column_lanes, picked), 0), groups) == iota((column_lanes, picked), 1)
    ).astype(BF16)
    same_group = (
        quotient(iota((column_lanes, features), 1), channels)
        == remainder(iota((column_lanes, features), 0), groups)
    )
    parts = []
    for k in range(3):
        keep = same_group
        if k == 0:
            keep = keep & (me > 0)
        if k == 2:
            keep = keep & (me < src_count - 1)
        parts.append(jnp.where(keep, dot(select, sbuf[k]), 0.0).astype(BF16))
    if width > 3 * column_lanes:
        parts.append(jnp.zeros((width - 3 * column_lanes, features), BF16))
    weights = jnp.concatenate(parts, axis=0)

    own[0].wait()
    for d in range(1, src_count):
        sends[d - 1].wait_recv()
        if tgt_count > 1:
            copy = forward(d, lambda column: buf.at[column, edge])
            copy.start()
            forwards.append(copy)
    def volume(chunk, place, keep):
        spots = [cols_ref[chunk * per_block + i] for i in range(per_block)]
        held, spot_rows = (buf, rows) if place is main else (rim, HALO)
        window = jnp.concatenate([held[spot] for spot in spots], axis=0)
        scores = lax.dot_general(
            window, weights, (((1,), (1,)), ((), ())), preferred_element_type=F32
        ) * (channels ** -0.5)
        scores = scores.reshape(per_block, spot_rows, width)
        if keep is not None:
            scores = jnp.where(keep, scores, 0.0)
        vol[pl.ds(chunk * per_block + 1, per_block), place, :] = scores.astype(BF16)

    def sums(chunk, place):
        window = jnp.concatenate(
            [
                vol[pl.ds(chunk * per_block + b, per_block), place, :].reshape(-1, width)
                for b in range(3)
            ],
            axis=1,
        )
        for a in range(3):
            acc[a, pl.ds(chunk * per_block, per_block), place, :] = dot(window, w1[a]).reshape(
                per_block, -1, width
            )

    def main_volume(chunk):
        volume(chunk, main, None)

    def main_sums(chunk):
        sums(chunk, main)

    def rim_volume(chunk):
        volume(chunk, arrived, in_rim)

    def at(ref, chunk, b):
        return ref[pl.ds(chunk * per_block + b, per_block)].reshape(chunk_rows, width)

    def shifted(parts):
        total = parts[1] + pltpu.roll(parts[0], 1, 0)
        return total + pltpu.roll(parts[2], chunk_rows - 1, 0)

    def middle_chunk(chunk):
        sums(chunk, arrived)
        one = shifted([at(acc.at[a], chunk, 0) for a in range(3)])
        one = jnp.maximum(one, 0.0).astype(BF16)
        two = jnp.maximum(dot(one, w2[...]), 0.0).reshape(per_block, span, width)
        two = jnp.where(valid_two, two, 0.0).astype(BF16)
        for b in range(3):
            lanes = slice(b * column_lanes, (b + 1) * column_lanes if b < 2 else width)
            sec[pl.ds(chunk * per_block + 2 - b, per_block), :, lanes] = two[:, :, lanes]

    def last_chunk(chunk):
        three = dot(at(sec, chunk, 1), w3[...])
        three = shifted([three[:, a * LANES : (a + 1) * LANES] for a in range(3)])
        stage[...] = jnp.maximum(three, 0.0)
        pieces = [
            stage[pl.ds(pl.multiple_of(i * span + half * HALO, HALO), rows), :]
            for i in range(per_block)
        ]
        rolled = []
        for d in range(window_rows):
            mixed = pieces[d % per_block]
            for j in range(1, per_block):
                mixed = jnp.where(in_group[j], pieces[(j + d) % per_block], mixed)
            rolled.append(pltpu.roll(mixed, d * groups, 1) if d else mixed)
        for h in range(window_rows):
            total = rolled[0]
            for d in range(1, window_rows):
                total = jnp.where(in_row[(d + h) % window_rows], rolled[d], total)
            out_ref[h, :, pl.ds(pl.multiple_of(chunk * LANES, LANES), LANES)] = total.astype(BF16)

    group = quotient(iota((rows, LANES), 1), groups)
    in_group = [group == j for j in range(per_block)]
    in_row = [remainder(group, window_rows) == h for h in range(window_rows)]

    for step in (main_volume, main_sums, rim_volume, middle_chunk, last_chunk):
        if step is rim_volume:
            for copy in forwards:
                copy.wait_recv()
        if chunks == 1:
            step(0)
        else:
            pl.loop(0, chunks)(step)

    pl.when(has_right)(to_right.wait_send)
    pl.when(has_left)(to_left.wait_send)
    for copy in sends:
        copy.wait_send()
    for copy in forwards:
        copy.wait_send()


def local(
    src_count,
    tgt_count,
    source_features,
    target_features,
    source_rows,
    target_cols,
    target_kernel_one,
    source_kernel,
    target_kernel_two,
):
    groups = source_kernel.shape[2]
    window_rows = source_rows.shape[0]
    breadth = target_cols.shape[0]
    map_rows, _, features = source_features.shape
    rows = target_features.shape[0]
    span = rows + HALO
    width = -(-3 * window_rows * groups // LANES) * LANES
    chunk_rows = LANES // groups * span
    taps = 9 * groups
    hbm = pl.BlockSpec(memory_space=pltpu.HBM)
    operands = (
        source_rows,
        target_cols,
        target_features[:, 0],
        source_features[:, 0],
        target_kernel_one.reshape(taps, groups),
        source_kernel.reshape(taps, groups),
        target_kernel_two.reshape(taps, groups),
    )
    dma = pltpu.SemaphoreType.DMA
    out = pl.pallas_call(
        functools.partial(kernel, src_count, tgt_count, breadth, window_rows, groups),
        out_shape=jax.ShapeDtypeStruct((window_rows, rows, breadth * groups), BF16),
        in_specs=[hbm] * 7,
        out_specs=pl.BlockSpec(memory_space=pltpu.VMEM),
        scratch_shapes=[
            pltpu.SMEM((window_rows,), jnp.int32),
            pltpu.SMEM((breadth,), jnp.int32),
            pltpu.VMEM((breadth, rows, features), BF16),
            pltpu.VMEM((map_rows, features), BF16),
            pltpu.VMEM((3, -(-window_rows // 16) * 16, features), BF16),
            pltpu.VMEM((3, taps, groups), BF16),
            pltpu.VMEM((breadth, HALO, features), BF16),
            pltpu.VMEM((breadth + 2, span, width), BF16),
            pltpu.VMEM((3, breadth, span, width), F32),
            pltpu.VMEM((breadth + 2, span, width), BF16),
            pltpu.VMEM((chunk_rows, LANES), F32),
            pltpu.VMEM((3, 3 * width, width), BF16),
            pltpu.VMEM((width, width), BF16),
            pltpu.VMEM((width, 3 * LANES), BF16),
            pltpu.VMEM((width, width), BF16),
            pltpu.VMEM((window_rows + 2, groups, width), BF16),
            dma((7,)),
            dma((src_count,)),
            dma((src_count,)),
            dma((src_count,)),
            dma((src_count,)),
            dma((2,)),
            dma((2,)),
        ],
        compiler_params=pltpu.CompilerParams(
            collective_id=0, has_side_effects=True, vmem_limit_bytes=48 * 1024 * 1024
        ),
    )(*(pltpu.with_memory_space_constraint(operand, pltpu.HBM) for operand in operands))
    return out[:, None]


def solution(mesh):
    return jax.shard_map(
        functools.partial(local, mesh.shape["src"], mesh.shape["tgt"]),
        mesh=mesh,
        in_specs=(
            P("pair", "src", None),
            P(("pair", "tgt"), "src", None),
            P("pair"),
            P("pair"),
            P(),
            P(),
            P(),
        ),
        out_specs=P("pair", "src", "tgt", None),
        check_vma=False,
    )
```

```python
import functools

import jax
import jax.numpy as jnp
from jax import lax
from jax.experimental import pallas as pl
from jax.experimental.pallas import tpu as pltpu
from jax.sharding import PartitionSpec as P

MESH = pl.DeviceIdType.MESH
LANES = 128
HALO = 16
BF16 = jnp.bfloat16
F32 = jnp.float32


def iota(shape, dim):
    return lax.broadcasted_iota(jnp.int32, shape, dim)


def quotient(x, n):
    return x >> (n.bit_length() - 1) if n & (n - 1) == 0 else x // n


def remainder(x, n):
    return x & (n - 1) if n & (n - 1) == 0 else x % n


def dot(a, b):
    return jnp.dot(a, b, preferred_element_type=F32)


def kernel(
    src_count,
    tgt_count,
    breadth,
    window_rows,
    groups,
    rows_hbm,
    cols_hbm,
    tgt_hbm,
    src_hbm,
    k1_hbm,
    ks_hbm,
    k2_hbm,
    out_ref,
    rows_ref,
    cols_ref,
    buf,
    sbuf,
    taps,
    rim,
    vol,
    acc,
    sec,
    stage,
    w1,
    w2,
    w3,
    diagonal,
    row_masks,
    local_sem,
    send_sem,
    recv_sem,
    halo_send,
    halo_recv,
    src_send,
    src_recv,
):
    rows, features = tgt_hbm.shape
    map_rows = src_hbm.shape[0]
    channels = features // groups
    span = rows + HALO
    width = vol.shape[2]
    column_lanes = window_rows * groups
    per_block = LANES // groups
    chunks = breadth // per_block
    chunk_rows = per_block * span
    me = lax.axis_index("src")
    half = lax.axis_index("tgt")
    main = pl.ds(pl.multiple_of(half * HALO, HALO), rows)

    def peer(d):
        return lax.rem(me + d, src_count)

    sbuf[0] = jnp.zeros(sbuf.shape[1:], BF16)
    sbuf[2] = jnp.zeros(sbuf.shape[1:], BF16)
    barrier = pltpu.get_barrier_semaphore()
    for d in range(1, src_count):
        pl.semaphore_signal(barrier, inc=1, device_id={"src": peer(d)}, device_id_type=MESH)
    if tgt_count > 1:
        pl.semaphore_signal(barrier, inc=1, device_id={"tgt": 1 - half}, device_id_type=MESH)

    own = [
        pltpu.make_async_copy(tgt_hbm, buf.at[me], local_sem.at[0]),
        pltpu.make_async_copy(src_hbm, sbuf.at[1], local_sem.at[1]),
        pltpu.make_async_copy(k1_hbm, taps.at[0], local_sem.at[2]),
        pltpu.make_async_copy(ks_hbm, taps.at[1], local_sem.at[3]),
        pltpu.make_async_copy(k2_hbm, taps.at[2], local_sem.at[4]),
        pltpu.make_async_copy(rows_hbm, rows_ref, local_sem.at[5]),
        pltpu.make_async_copy(cols_hbm, cols_ref, local_sem.at[6]),
    ]
    for copy in own:
        copy.start()
    zero_block = jnp.zeros((span, width), BF16)
    vol[0] = zero_block
    vol[breadth + 1] = zero_block
    sec[1] = zero_block
    sec[breadth] = zero_block
    expand = (remainder(iota((groups, width), 1), groups) == iota((groups, width), 0)).astype(BF16)
    lane_group = quotient(iota((groups, width), 1), groups)
    lane_row = remainder(lane_group, window_rows)
    nothing = jnp.zeros((groups, width), BF16)

    one = jnp.ones((groups, width), BF16)
    for j in range(width // groups):
        diagonal[pl.ds(j * groups, groups), :] = jnp.where(lane_group == j, one, nothing)
    for h in range(-1, window_rows + 1):
        row_masks[h + 1] = jnp.where(lane_row == h, one, nothing)
    pl.semaphore_wait(barrier, src_count - 1 + (1 if tgt_count > 1 else 0))

    edge = pl.ds(pl.multiple_of((1 - half) * (rows - HALO), HALO), HALO)
    arrived = pl.ds(pl.multiple_of((1 - half) * rows, HALO), HALO)

    to_right = pltpu.make_async_remote_copy(
        src_ref=src_hbm, dst_ref=sbuf.at[0], send_sem=src_send.at[0], recv_sem=src_recv.at[0],
        device_id={"src": lax.rem(me + 1, src_count)}, device_id_type=MESH,
    )
    to_left = pltpu.make_async_remote_copy(
        src_ref=src_hbm, dst_ref=sbuf.at[2], send_sem=src_send.at[1], recv_sem=src_recv.at[1],
        device_id={"src": lax.rem(me + src_count - 1, src_count)}, device_id_type=MESH,
    )
    sends = []
    for d in range(1, src_count):
        sends.append(
            pltpu.make_async_remote_copy(
                src_ref=tgt_hbm, dst_ref=buf.at[me], send_sem=send_sem.at[d],
                recv_sem=recv_sem.at[d], device_id={"src": peer(d)}, device_id_type=MESH,
            )
        )
    order = sorted(range(1, src_count), key=lambda d: -min(d, src_count - d))
    has_left, has_right = me > 0, me < src_count - 1
    pl.when(has_right)(to_right.start)
    pl.when(has_left)(to_left.start)
    for d in order:
        sends[d - 1].start()

    def forward(d, source):
        column = lax.rem(me + src_count - d, src_count)
        return pltpu.make_async_remote_copy(
            src_ref=source(column), dst_ref=rim.at[column], send_sem=halo_send.at[d],
            recv_sem=halo_recv.at[d], device_id={"tgt": 1 - half}, device_id_type=MESH,
        )

    forwards = []
    if tgt_count == 1:
        for column in range(breadth):
            rim[column] = jnp.zeros((HALO, features), BF16)
    else:
        offset = pl.multiple_of((1 - half) * (rows - HALO), HALO)
        forwards.append(forward(0, lambda column: tgt_hbm.at[pl.ds(offset, HALO)]))
        forwards[0].start()

    for copy in own[2:5]:
        copy.wait()
    spread = [dot(taps[i], expand).astype(BF16) for i in range(3)]
    def tap(i, a, b):
        start = (a * 3 + b) * groups
        return spread[i][start : start + groups]

    for a in range(3):
        for b in range(3):
            for j in range(width // groups):
                w1[a, pl.ds(b * width + j * groups, groups), :] = (
                    tap(0, a, b) * diagonal[pl.ds(j * groups, groups), :]
                )
    for j in range(width // groups):
        k, h = divmod(j, window_rows)
        two = nothing
        three = [nothing[:, :LANES]] * 3
        if k < 3:
            for a in range(3):
                two = two + tap(1, a, k) * row_masks[h - a + 2]
                three[a] = tap(2, a, k)[:, :LANES] * row_masks[h + 1][:, :LANES]
        w2[pl.ds(j * groups, groups), :] = two
        for a in range(3):
            w3[pl.ds(j * groups, groups), pl.ds(a * LANES, LANES)] = three[a]

    def valid(extra):
        position = iota((span, width), 0)
        low = half * (HALO - extra)
        return ((position >= low) & (position < low + rows + extra))[None]

    valid_two = valid(1)
    first_kept = half * (HALO - 2)
    rim_position = iota((HALO, width), 0)
    in_rim = ((rim_position >= first_kept) & (rim_position < first_kept + 2))[None]

    pl.when(has_left)(to_right.wait_recv)
    pl.when(has_right)(to_left.wait_recv)
    own[1].wait()
    own[5].wait()
    own[6].wait()
    row_of = quotient(iota((column_lanes, map_rows), 0), groups)
    wanted = jnp.zeros((column_lanes, map_rows), jnp.int32)
    for h in range(window_rows):
        wanted = jnp.where(row_of == h, rows_ref[h], wanted)
    select = (iota((column_lanes, map_rows), 1) == wanted).astype(BF16)
    same_group = (
        quotient(iota((column_lanes, features), 1), channels)
        == remainder(iota((column_lanes, features), 0), groups)
    )
    parts = []
    for k in range(3):
        keep = same_group
        if k == 0:
            keep = keep & (me > 0)
        if k == 2:
            keep = keep & (me < src_count - 1)
        parts.append(jnp.where(keep, dot(select, sbuf[k]), 0.0).astype(BF16))
    if width > 3 * column_lanes:
        parts.append(jnp.zeros((width - 3 * column_lanes, features), BF16))
    weights = jnp.concatenate(parts, axis=0)

    own[0].wait()
    for d in range(1, src_count):
        sends[d - 1].wait_recv()
        if tgt_count > 1:
            copy = forward(d, lambda column: buf.at[column, edge])
            copy.start()
            forwards.append(copy)
    def volume(chunk, place, keep):
        spots = [cols_ref[chunk * per_block + i] for i in range(per_block)]
        held, spot_rows = (buf, rows) if place is main else (rim, HALO)
        window = jnp.concatenate([held[spot] for spot in spots], axis=0)
        scores = lax.dot_general(
            window, weights, (((1,), (1,)), ((), ())), preferred_element_type=F32
        ) * (channels ** -0.5)
        scores = scores.reshape(per_block, spot_rows, width)
        if keep is not None:
            scores = jnp.where(keep, scores, 0.0)
        vol[pl.ds(chunk * per_block + 1, per_block), place, :] = scores.astype(BF16)

    def sums(chunk, place):
        window = jnp.concatenate(
            [
                vol[pl.ds(chunk * per_block + b, per_block), place, :].reshape(-1, width)
                for b in range(3)
            ],
            axis=1,
        )
        for a in range(3):
            acc[a, pl.ds(chunk * per_block, per_block), place, :] = dot(window, w1[a]).reshape(
                per_block, -1, width
            )

    def main_volume(chunk):
        volume(chunk, main, None)

    def main_sums(chunk):
        sums(chunk, main)

    def rim_volume(chunk):
        volume(chunk, arrived, in_rim)

    def at(ref, chunk, b):
        return ref[pl.ds(chunk * per_block + b, per_block)].reshape(chunk_rows, width)

    def shifted(parts):
        total = parts[1] + pltpu.roll(parts[0], 1, 0)
        return total + pltpu.roll(parts[2], chunk_rows - 1, 0)

    def middle_chunk(chunk):
        sums(chunk, arrived)
        one = shifted([at(acc.at[a], chunk, 0) for a in range(3)])
        one = jnp.maximum(one, 0.0).astype(BF16)
        two = jnp.maximum(dot(one, w2[...]), 0.0).reshape(per_block, span, width)
        two = jnp.where(valid_two, two, 0.0).astype(BF16)
        for b in range(3):
            lanes = slice(b * column_lanes, (b + 1) * column_lanes if b < 2 else width)
            sec[pl.ds(chunk * per_block + 2 - b, per_block), :, lanes] = two[:, :, lanes]

    def last_chunk(chunk):
        three = dot(at(sec, chunk, 1), w3[...])
        three = shifted([three[:, a * LANES : (a + 1) * LANES] for a in range(3)])
        stage[...] = jnp.maximum(three, 0.0)
        pieces = [
            stage[pl.ds(pl.multiple_of(i * span + half * HALO, HALO), rows), :]
            for i in range(per_block)
        ]
        rolled = []
        for d in range(window_rows):
            mixed = pieces[d % per_block]
            for j in range(1, per_block):
                mixed = jnp.where(in_group[j], pieces[(j + d) % per_block], mixed)
            rolled.append(pltpu.roll(mixed, d * groups, 1) if d else mixed)
        for h in range(window_rows):
            total = rolled[0]
            for d in range(1, window_rows):
                total = jnp.where(in_row[(d + h) % window_rows], rolled[d], total)
            out_ref[h, :, pl.ds(pl.multiple_of(chunk * LANES, LANES), LANES)] = total.astype(BF16)

    group = quotient(iota((rows, LANES), 1), groups)
    in_group = [group == j for j in range(per_block)]
    in_row = [remainder(group, window_rows) == h for h in range(window_rows)]

    for step in (main_volume, main_sums, rim_volume, middle_chunk, last_chunk):
        if step is rim_volume:
            for copy in forwards:
                copy.wait_recv()
        if chunks == 1:
            step(0)
        else:
            pl.loop(0, chunks)(step)

    pl.when(has_right)(to_right.wait_send)
    pl.when(has_left)(to_left.wait_send)
    for copy in sends:
        copy.wait_send()
    for copy in forwards:
        copy.wait_send()


def local(
    src_count,
    tgt_count,
    source_features,
    target_features,
    source_rows,
    target_cols,
    target_kernel_one,
    source_kernel,
    target_kernel_two,
):
    groups = source_kernel.shape[2]
    window_rows = source_rows.shape[0]
    breadth = target_cols.shape[0]
    map_rows, _, features = source_features.shape
    rows = target_features.shape[0]
    span = rows + HALO
    width = -(-3 * window_rows * groups // LANES) * LANES
    chunk_rows = LANES // groups * span
    taps = 9 * groups
    hbm = pl.BlockSpec(memory_space=pltpu.HBM)
    operands = (
        source_rows,
        target_cols,
        target_features[:, 0],
        source_features[:, 0],
        target_kernel_one.reshape(taps, groups),
        source_kernel.reshape(taps, groups),
        target_kernel_two.reshape(taps, groups),
    )
    dma = pltpu.SemaphoreType.DMA
    out = pl.pallas_call(
        functools.partial(kernel, src_count, tgt_count, breadth, window_rows, groups),
        out_shape=jax.ShapeDtypeStruct((window_rows, rows, breadth * groups), BF16),
        in_specs=[hbm] * 7,
        out_specs=pl.BlockSpec(memory_space=pltpu.VMEM),
        scratch_shapes=[
            pltpu.SMEM((window_rows,), jnp.int32),
            pltpu.SMEM((breadth,), jnp.int32),
            pltpu.VMEM((breadth, rows, features), BF16),
            pltpu.VMEM((3, map_rows, features), BF16),
            pltpu.VMEM((3, taps, groups), BF16),
            pltpu.VMEM((breadth, HALO, features), BF16),
            pltpu.VMEM((breadth + 2, span, width), BF16),
            pltpu.VMEM((3, breadth, span, width), F32),
            pltpu.VMEM((breadth + 2, span, width), BF16),
            pltpu.VMEM((chunk_rows, LANES), F32),
            pltpu.VMEM((3, 3 * width, width), BF16),
            pltpu.VMEM((width, width), BF16),
            pltpu.VMEM((width, 3 * LANES), BF16),
            pltpu.VMEM((width, width), BF16),
            pltpu.VMEM((window_rows + 2, groups, width), BF16),
            dma((7,)),
            dma((src_count,)),
            dma((src_count,)),
            dma((src_count,)),
            dma((src_count,)),
            dma((2,)),
            dma((2,)),
        ],
        compiler_params=pltpu.CompilerParams(
            collective_id=0, has_side_effects=True, vmem_limit_bytes=48 * 1024 * 1024
        ),
    )(*(pltpu.with_memory_space_constraint(operand, pltpu.HBM) for operand in operands))
    return out[:, None]


def solution(mesh):
    return jax.shard_map(
        functools.partial(local, mesh.shape["src"], mesh.shape["tgt"]),
        mesh=mesh,
        in_specs=(
            P("pair", "src", None),
            P(("pair", "tgt"), "src", None),
            P("pair"),
            P("pair"),
            P(),
            P(),
            P(),
        ),
        out_specs=P("pair", "src", "tgt", None),
        check_vma=False,
    )
```
